32 devices in a mesh: gx: 4 (over y, core), gy: 8 (over z, x).
Axes of the slice: x: 2, y: 2, z: 4, core: 2. Of those that a mesh axis runs over, the one named last changes fastest.
Arguments:
- start_vector: float32 [2, 16, 64, 1024], P(None, None, 'gx', 'gy'), may hold values from -6 to 6
- viscosity: float32 [16, 64, 1024], P(None, 'gx', 'gy'), may hold values from 0.1 to 10
- friction: float32 [16, 64, 1024], P(None, 'gx', 'gy'), may hold values from 0.5 to 5
- shifts: float32 [8], replicated, may hold values from 0.2 to 1.6, as said below
Outputs:
- orthonormal: float32 [9, 2, 16, 64, 1024], P(None, None, None, 'gx', 'gy')
- factor: float32 [9, 9], replicated
The draws below stay inside these ranges and needn't reach their ends.
Inputs may be any that keep to these rules, and one draw needn't show every extreme that they name: The 8 shifts are distinct, one in each of 8 equal parts of the range.
All inputs are finite; a program needn't handle non-finite values.
Results may differ from the reference program's by a relative error of at most 0.00035.
Values sent between devices are 32-bit elements; how exact they have to be, the bound alone decides.
A program may use at most 128 MiB of HBM per device.

```python
import math
import jax
import jax.numpy as jnp
from jax import lax

NZ = 16
S = 8
NX = 64
NY = 1024
M = 2097152


def draw_start_vector(key, part):
    first_key = jax.random.fold_in(key, 11)
    shape_full = (2, NZ, NX, NY)
    values = jax.random.normal(first_key, shape_full, jnp.float32)
    return jnp.clip(values, -6.0, 6.0).astype(jnp.float32)


def draw_shifts(key, part):
    jitter_key = jax.random.fold_in(key, 21)
    order_key = jax.random.fold_in(key, 22)
    jitter = jax.random.uniform(jitter_key, (S,), jnp.float32, 0.1, 0.9)
    spaced = 0.2 + 1.4 * (jnp.arange(S).astype(jnp.float32) + jitter) / S
    order = jax.random.permutation(order_key, S)
    return spaced[order].astype(jnp.float32)


def steps_of(rng, shape, pieces, least, top_value):
    gain = 1.0
    for dim, parts in pieces:
        draws = jax.random.uniform(jax.random.fold_in(jax.random.fold_in(rng, 6), dim), (parts,), jnp.float32, least / len(pieces), top_value / len(pieces))
        gain = gain * jnp.repeat(jnp.exp(draws), shape[dim] // parts).reshape((-1,) + (1,) * (len(shape) - 1 - dim))
    return gain


def setup_inputs(seed: int = 0) -> dict:
    key_of = jax.random.split(jax.random.key(seed), 5)
    start_vector = draw_start_vector(jax.random.fold_in(key_of[4], 71), 0)
    viscosity = jnp.clip(jnp.exp(math.log(10.0) - 4.6051702 * jax.random.uniform(key_of[1], (NZ, NX, NY), jnp.float32) ** steps_of(key_of[1], (NZ, NX, NY), ((1, 4), (2, 8)), -0.2, 0.2)), 0.1, 10.0)
    friction = jnp.clip(jnp.exp(math.log(5.0) - 2.3025851 * jax.random.uniform(key_of[2], (NZ, NX, NY), jnp.float32) ** steps_of(key_of[2], (NZ, NX, NY), ((1, 4), (2, 8)), -0.2, 0.2)), 0.5, 5.0)
    shifts = draw_shifts(jax.random.fold_in(key_of[4], 71), 0)
    return dict(start_vector=start_vector, viscosity=viscosity, friction=friction, shifts=shifts)


cross_gain = 1.0

def neighbour_offsets():
    offsets = []
    for shift_z in (-1, 0, 1):
        for shift_x in (-1, 0, 1):
            for shift_y in (-1, 0, 1):
                distance = abs(shift_z) + abs(shift_x) + abs(shift_y)
                if distance == 0:
                    continue
                offsets.append((shift_z, shift_x, shift_y, 0.5 ** (distance - 1)))
    return offsets

def apply_operator(field_pad, eta_pad, friction, region_mask):
    levels = friction.shape[0]
    row_count = field_pad.shape[2] - 2
    col_count = field_pad.shape[3] - 2
    eta_z = jnp.pad(eta_pad, ((1, 1), (0, 0), (0, 0)))
    field_z = jnp.pad(field_pad, ((0, 0), (1, 1), (0, 0), (0, 0)))
    centre_eta = eta_pad[:, 1:1 + row_count, 1:1 + col_count]
    diagonal = friction
    summed = jnp.zeros((2, levels, row_count, col_count), jnp.float32)
    for shift_z, shift_x, shift_y, weight in neighbour_offsets():
        linkage = weight * 0.5 * (centre_eta + eta_z[1 + shift_z:1 + shift_z + levels, 1 + shift_x:1 + shift_x + row_count, 1 + shift_y:1 + shift_y + col_count])
        diagonal = diagonal + linkage
        summed = summed + linkage[None] * field_z[:, 1 + shift_z:1 + shift_z + levels, 1 + shift_x:1 + shift_x + row_count, 1 + shift_y:1 + shift_y + col_count]
    crossed = 0.25 * (field_pad[:, :, 2:2 + row_count, 2:2 + col_count] - field_pad[:, :, 2:2 + row_count, 0:col_count] - field_pad[:, :, 0:row_count, 2:2 + col_count] + field_pad[:, :, 0:row_count, 0:col_count])
    centre = field_pad[:, :, 1:1 + row_count, 1:1 + col_count]
    safe_diag = jnp.where(region_mask > 0, diagonal, 1.0)
    result = centre - (summed - cross_gain * centre_eta[None] * crossed[::-1]) / safe_diag
    return result * region_mask

def lower_inverse(factor_low):
    order_n = factor_low.shape[0]
    identity = jnp.eye(order_n, dtype=jnp.float32)
    inverse = jnp.zeros((order_n, order_n), jnp.float32)
    for position in range(order_n):
        earlier = jnp.dot(factor_low[position, :position], inverse[:position], precision=lax.Precision.HIGHEST)
        inverse = inverse.at[position].set((identity[position] - earlier) / factor_low[position, position])
    return inverse

def cholesky_pass(basis_rows, gram):
    factor_low = jnp.linalg.cholesky(gram)
    return (jnp.dot(lower_inverse(factor_low), basis_rows, precision=lax.Precision.HIGHEST), factor_low)

def reference(start_vector, viscosity, friction, shifts):
    current = start_vector
    krylov = [start_vector]
    eta_pad = jnp.pad(viscosity, ((0, 0), (1, 1), (1, 1)))
    for power in range(S):
        padded = jnp.pad(current, ((0, 0), (0, 0), (1, 1), (1, 1)))
        current = apply_operator(padded, eta_pad, friction, 1.0) - shifts[power] * current
        krylov.append(current)
    basis_rows = jnp.stack(krylov).reshape(S + 1, -1)
    gram_one = jnp.dot(basis_rows, basis_rows.T, precision=lax.Precision.HIGHEST) / M
    ortho_one, low_one = cholesky_pass(basis_rows, gram_one)
    gram_two = jnp.dot(ortho_one, ortho_one.T, precision=lax.Precision.HIGHEST) / M
    ortho_two, low_two = cholesky_pass(ortho_one, gram_two)
    factor = jnp.dot(low_two.T, low_one.T, precision=lax.Precision.HIGHEST)
    return (ortho_two.reshape(S + 1, 2, NZ, NX, NY), factor)
```

```python
import functools

import jax
import jax.numpy as jnp
from jax import lax
from jax.experimental import pallas as pl
from jax.experimental.pallas import tpu as pltpu
from jax.sharding import PartitionSpec as P

MESH = pl.DeviceIdType.MESH
HALO = 8
GROUP = 2 * HALO
DIRECTIONS = ((1, 0), (-1, 0), (0, 1), (0, -1), (1, 1), (1, -1), (-1, 1), (-1, -1))


def both(lower_ok, upper_ok):
    if lower_ok is None:
        return upper_ok
    if upper_ok is None:
        return lower_ok
    return jnp.logical_and(lower_ok, upper_ok)


def kernel(
    gx_count,
    gy_count,
    start_hbm,
    eta_hbm,
    fric_hbm,
    shift_hbm,
    out_ref,
    factor_ref,
    lower_inv,
    start_ref,
    eta_in_ref,
    fric_in_ref,
    shift_ref,
    load_sem,
    cur,
    eta,
    fric,
    centre_coef,
    a_mid,
    g_mid,
    a_up,
    g_up,
    a_down,
    g_down,
    packed,
    edge,
    red,
    mine,
    slots,
    splat,
    row_send,
    row_recv,
    pack_send,
    pack_recv,
    gram_send,
    gram_recv,
):
    powers = shift_hbm.shape[0]
    count = powers + 1
    levels, rows, lanes = eta_in_ref.shape
    wide = rows + 2 * HALO
    me_x, me_y = lax.axis_index("gx"), lax.axis_index("gy")
    total_count = 2.0 * levels * rows * lanes * gx_count * gy_count

    def exists(dx, dy):
        x_ok = {1: me_x < gx_count - 1, -1: me_x > 0, 0: None}[dx]
        y_ok = {1: me_y < gy_count - 1, -1: me_y > 0, 0: None}[dy]
        return both(x_ok, y_ok)

    def device(dx, dy):
        return (jnp.clip(me_x + dx, 0, gx_count - 1), jnp.clip(me_y + dy, 0, gy_count - 1))

    devices = gx_count * gy_count
    me = me_x * gy_count + me_y

    def peer(step):
        other = lax.rem(me + step, devices)
        return (lax.div(other, gy_count), lax.rem(other, gy_count))

    barrier = pltpu.get_barrier_semaphore()
    for step in range(1, devices):
        pl.semaphore_signal(barrier, inc=1, device_id=peer(step), device_id_type=MESH)
    loads = [
        pltpu.make_async_copy(src, dst, load_sem.at[n])
        for n, (src, dst) in enumerate(
            (
                (start_hbm, start_ref),
                (eta_hbm, eta_in_ref),
                (fric_hbm, fric_in_ref),
                (shift_hbm, shift_ref),
            )
        )
    ]
    for load in loads:
        load.start()
    for load in loads:
        load.wait()

    lane = lax.broadcasted_iota(jnp.int32, (wide, lanes), 1)
    row = lax.broadcasted_iota(jnp.int32, (wide, lanes), 0)
    lane_in = lane[:rows]

    def source(field, level):
        if field < 2:
            return start_ref[field, level]
        return (eta_in_ref, fric_in_ref)[field - 2][level]

    for field in range(4):
        for group in range(levels // 8):
            tile = jnp.zeros((rows, lanes), jnp.float32)
            for inner in range(8):
                turned = pltpu.roll(
                    source(field, group * 8 + inner), (GROUP * inner + HALO) % lanes, 1
                )
                tile = jnp.where(lane_in // GROUP == inner, turned, tile)
            packed[field * (levels // 8) + group] = tile

    pl.semaphore_wait(barrier, devices - 1)

    def row_copies(index):
        dx, dy = DIRECTIONS[index]
        src = pl.ds(rows - HALO, HALO) if dx > 0 else pl.ds(0, HALO)
        dst = pl.ds(0, HALO) if dx > 0 else pl.ds(rows + HALO, HALO)
        inner = pl.ds(1, levels)
        pairs = (
            (start_ref.at[:, :, src], cur.at[0, 0, :, inner, dst]),
            (eta_in_ref.at[:, src], eta.at[0, inner, dst]),
            (fric_in_ref.at[:, src], fric.at[0, :, dst]),
        )
        return [
            pltpu.make_async_remote_copy(
                src_ref=a,
                dst_ref=b,
                send_sem=row_send.at[index, n],
                recv_sem=row_recv.at[index, n],
                device_id=device(dx, dy),
                device_id_type=MESH,
            )
            for n, (a, b) in enumerate(pairs)
        ]

    def pack_copies(index):
        dx, dy = DIRECTIONS[index]
        side = 0 if dy > 0 else 1
        if dx == 0:
            src, dst = pl.ds(0, rows), pl.ds(HALO, rows)
        elif dx > 0:
            src, dst = pl.ds(rows - HALO, HALO), pl.ds(0, HALO)
        else:
            src, dst = pl.ds(0, HALO), pl.ds(rows + HALO, HALO)
        return [
            pltpu.make_async_remote_copy(
                src_ref=packed.at[:, src],
                dst_ref=edge.at[side, :, dst],
                send_sem=pack_send.at[index - 2],
                recv_sem=pack_recv.at[index - 2],
                device_id=device(dx, dy),
                device_id_type=MESH,
            )
        ]

    def copies(index):
        return row_copies(index) if index < 2 else pack_copies(index)

    for index, (dx, dy) in enumerate(DIRECTIONS):

        @pl.when(exists(dx, dy))
        def _():
            for copy in copies(index):
                copy.start()

    zero_tile = jnp.zeros((wide, lanes), jnp.float32)
    for comp in range(2):
        for tile in range(2):
            for slot in range(2):
                cur[slot, tile, comp, 0] = zero_tile
                cur[slot, tile, comp, levels + 1] = zero_tile
        cur[0, 0, comp, 1 : levels + 1, HALO : HALO + rows] = start_ref[comp]
        out_ref[0, comp] = start_ref[comp]
    for tile in range(2):
        eta[tile, 0] = zero_tile
        eta[tile, levels + 1] = zero_tile
    eta[0, 1 : levels + 1, HALO : HALO + rows] = eta_in_ref[...]
    fric[0, :, HALO : HALO + rows] = fric_in_ref[...]
    for index, (dx, dy) in enumerate(DIRECTIONS):
        here = exists(-dx, -dy)

        @pl.when(jnp.logical_not(here))
        def _():
            start = 0 if dx > 0 else (HALO if dx == 0 else rows + HALO)
            size = rows if dx == 0 else HALO
            if dy == 0:
                blank = jnp.zeros((levels, HALO, lanes), jnp.float32)
                for comp in range(2):
                    cur[0, 0, comp, 1 : levels + 1, start : start + size] = blank
                eta[0, 1 : levels + 1, start : start + size] = blank
                fric[0, :, start : start + size] = blank
            else:
                side = 0 if dy > 0 else 1
                edge[side, :, start : start + size] = jnp.zeros(
                    (edge.shape[1], size, lanes), jnp.float32
                )

        @pl.when(here)
        def _():
            for copy in copies(index):
                copy.wait_recv()

    is_edge = (lane < HALO) | (lane >= lanes - HALO)
    for field in range(4):
        for group in range(levels // 8):
            spot = field * (levels // 8) + group
            merged = jnp.where(lane % GROUP >= HALO, edge[1, spot], edge[0, spot])
            for inner in range(8):
                level = group * 8 + inner
                turned = pltpu.roll(merged, (2 * lanes - GROUP * inner - HALO) % lanes, 1)
                turned = jnp.where(is_edge, turned, 0.0)
                if field < 2:
                    cur[0, 1, field, level + 1] = turned
                elif field == 2:
                    eta[1, level + 1] = turned
                else:
                    fric[1, level] = turned

    def from_next(first, second):
        a, b = pltpu.roll(first, lanes - 1, 1), pltpu.roll(second, lanes - 1, 1)
        at_end = lane[: first.shape[0]] == lanes - 1
        return jnp.where(at_end, b, a), jnp.where(at_end, a, b)

    def from_last(first, second):
        a, b = pltpu.roll(first, 1, 1), pltpu.roll(second, 1, 1)
        at_start = lane[: first.shape[0]] == 0
        return jnp.where(at_start, b, a), jnp.where(at_start, a, b)

    def smooth_rows(value):
        pair = value + pltpu.roll(value, wide - 1, 0)
        return pair + pltpu.roll(pair, 1, 0)

    row_ok = ((row >= HALO) | (me_x > 0)) & ((row < HALO + rows) | (me_x < gx_count - 1))
    side_ok = ((lane < HALO) & (me_y < gy_count - 1)) | ((lane >= lanes - HALO) & (me_y > 0))
    inside = (row_ok, row_ok & side_ok)

    def coefficients(level, carry):
        sums = [
            smooth_rows(eta[t, level] + 2.0 * eta[t, level + 1] + eta[t, level + 2])
            for t in range(2)
        ]
        after, before = from_next(*sums), from_last(*sums)
        a_pair, g_pair = [], []
        for t in range(2):
            here = eta[t, level + 1]
            diagonal = (
                fric[t, level] + 6.0 * here + 0.125 * (2.0 * sums[t] + after[t] + before[t])
            )
            inverse = jnp.where(inside[t], 0.125 / jnp.where(inside[t], diagonal, 1.0), 0.0)
            a_pair.append(here * inverse)
            g_pair.append(inverse)
            centre_coef[t, level] = 1.0 + 16.0 * a_pair[t]
            a_mid[t, level] = 2.0 * a_pair[t]
            g_mid[t, level] = 2.0 * g_pair[t]
        for values, up, down in ((a_pair, a_up, a_down), (g_pair, g_up, g_down)):
            ahead, behind = from_last(*values), from_next(*values)
            for t in range(2):
                up[t, level] = ahead[t]
                down[t, level] = behind[t]
        return carry

    lax.fori_loop(0, levels, coefficients, 0)

    def power_step(power, carry, final=False):
        kept = slice(HALO, HALO + rows) if final else slice(0, wide)

        slot = power % 2
        newton = shift_ref[power]

        def level_step(level, inner_carry):
            crossed = [[None, None], [None, None]]
            for t in range(2):
                for comp in range(2):
                    value = cur[slot, t, comp, level + 1]
                    slope = pltpu.roll(value, wide - 1, 0) - pltpu.roll(value, 1, 0)
                    crossed[comp][t] = (slope + slope)[kept]
            for comp in range(2):
                centre, ups, downs = [], [], []
                for t in range(2):
                    below = cur[slot, t, comp, level]
                    value = cur[slot, t, comp, level + 1]
                    above = cur[slot, t, comp, level + 2]
                    plain = smooth_rows(below + 2.0 * value + above)[kept]
                    scaled = smooth_rows(
                        eta[t, level] * below
                        + 2.0 * (eta[t, level + 1] * value)
                        + eta[t, level + 2] * above
                    )[kept]
                    cross = crossed[1 - comp][t]
                    centre.append(
                        (centre_coef[t, level, kept] - newton) * value[kept]
                        - (a_mid[t, level, kept] * plain + g_mid[t, level, kept] * scaled)
                    )
                    ups.append(a_up[t, level, kept] * (plain - cross) + g_up[t, level, kept] * scaled)
                    downs.append(a_down[t, level, kept] * (plain + cross) + g_down[t, level, kept] * scaled)
                after, before = from_next(*ups), from_last(*downs)
                for t in range(2):
                    result = centre[t] - (after[t] + before[t])
                    if not final:
                        cur[1 - slot, t, comp, level + 1] = result
                    if final and t == 0:
                        out_ref[power + 1, comp, level] = result
                    elif t == 0:
                        out_ref[power + 1, comp, level] = result[HALO : HALO + rows]
            return inner_carry

        return lax.fori_loop(0, levels, level_step, carry)

    lax.fori_loop(0, powers - 1, power_step, 0)
    power_step(powers - 1, 0, final=True)

    pairs = [(i, j) for i in range(count) for j in range(i + 1)]
    place = {pair: n for n, pair in enumerate(pairs)}
    padded = red.shape[0]
    red[...] = jnp.zeros((padded, lanes), jnp.float32)
    ones = jnp.ones((8, lanes), jnp.float32)
    splat_rows = splat.shape[0]
    diagonal = lax.broadcasted_iota(jnp.int32, (splat_rows, lanes), 1) == lax.broadcasted_iota(
        jnp.int32, (splat_rows, lanes), 0
    )

    def add_products(sums, vectors):
        return tuple(total + vectors[i] * vectors[j] for total, (i, j) in zip(sums, pairs))

    zeros = tuple(jnp.zeros((8, lanes), jnp.float32) for _ in pairs)

    def gram_of(sums, phase):
        for n, total in enumerate(sums):
            red[n : n + 1] = jnp.sum(total, axis=0, keepdims=True)
        mine[phase] = lax.dot_general(
            ones,
            red[...],
            (((1,), (1,)), ((), ())),
            precision=lax.Precision.HIGHEST,
            preferred_element_type=jnp.float32,
        )
        for step in range(1, devices):
            pltpu.make_async_remote_copy(
                src_ref=mine.at[phase, pl.ds(0, 1)],
                dst_ref=slots.at[phase, pl.ds(me, 1)],
                send_sem=gram_send.at[phase],
                recv_sem=gram_recv.at[phase],
                device_id=peer(step),
                device_id_type=MESH,
            ).start()
        slots[phase, pl.ds(me, 1)] = mine[phase, 0:1]
        every = pltpu.make_async_remote_copy(
            src_ref=slots.at[phase, pl.ds(0, devices - 1)],
            dst_ref=slots.at[phase, pl.ds(0, devices - 1)],
            send_sem=gram_send.at[phase],
            recv_sem=gram_recv.at[phase],
            device_id=peer(1),
            device_id_type=MESH,
        )
        every.wait_recv()
        whole = jnp.sum(slots[phase], axis=0, keepdims=True) / total_count
        spread = jnp.where(diagonal, jnp.broadcast_to(whole, diagonal.shape), 0.0)
        splat[...] = jnp.broadcast_to(jnp.sum(spread, axis=1, keepdims=True), spread.shape)
        every.wait_send()
        return {pair: splat[n : n + 1] for n, pair in enumerate(pairs)}

    def factorise(gram):
        left = dict(gram)
        low, inv = {}, {}
        for j in range(count):
            root = jnp.sqrt(left[j, j])
            scale = 1.0 / root
            low[j, j], inv[j, j] = root, scale
            for i in range(j + 1, count):
                low[i, j] = left[i, j] * scale
            for i in range(j + 1, count):
                for k in range(j + 1, i + 1):
                    left[i, k] = left[i, k] - low[i, j] * low[k, j]
        for i in range(count):
            for j in range(i):
                total = low[i, j] * inv[j, j]
                for k in range(j + 1, i):
                    total = total + low[i, k] * inv[k, j]
                inv[i, j] = -(total * inv[i, i])
        for pair, n in place.items():
            lower_inv[n : n + 1] = inv[pair]
        return low

    def combine(vectors):
        results = []
        for i in range(count):
            total = lower_inv[place[i, 0] : place[i, 0] + 1] * vectors[0]
            for j in range(1, i + 1):
                total = total + lower_inv[place[i, j] : place[i, j] + 1] * vectors[j]
            results.append(total)
        return results

    def basis_at(spot, half):
        comp, level = spot // levels, lax.rem(spot, levels)
        return [out_ref[n, comp, level, 8 * half : 8 * half + 8] for n in range(count)]

    def gram_step(spot, sums):
        for half in range(rows // 8):
            sums = add_products(sums, basis_at(spot, half))
        return sums

    low_one = factorise(gram_of(lax.fori_loop(0, 2 * levels, gram_step, zeros), 0))

    def ortho_step(spot, sums):
        comp, level = spot // levels, lax.rem(spot, levels)
        for half in range(rows // 8):
            vectors = combine(basis_at(spot, half))
            for n in range(count):
                out_ref[n, comp, level, 8 * half : 8 * half + 8] = vectors[n]
            sums = add_products(sums, vectors)
        return sums

    low_two = factorise(gram_of(lax.fori_loop(0, 2 * levels, ortho_step, zeros), 1))

    fac_row = lax.broadcasted_iota(jnp.int32, (count, count), 0)
    fac_col = lax.broadcasted_iota(jnp.int32, (count, count), 1)
    factor = jnp.zeros((count, count), jnp.float32)
    for i in range(count):
        for j in range(i, count):
            total = low_two[i, i] * low_one[j, i]
            for k in range(i + 1, j + 1):
                total = total + low_two[k, i] * low_one[j, k]
            factor = jnp.where((fac_row == i) & (fac_col == j), total[:, :count], factor)
    factor_ref[...] = factor

    for index, (dx, dy) in enumerate(DIRECTIONS):

        @pl.when(exists(dx, dy))
        def _():
            for copy in copies(index):
                copy.wait_send()


def finish(inverse_ref, basis_ref, factor_in, out_ref, factor_ref):
    count, _, depth, rows, _ = out_ref.shape
    comp, first = pl.program_id(0), pl.program_id(1) * depth
    factor_ref[...] = factor_in[...]

    def one_level(level, carry):
        for half in range(rows // 8):
            part = slice(8 * half, 8 * half + 8)
            vectors = [basis_ref[n, comp, first + level, part] for n in range(count)]
            spot = 0
            for i in range(count):
                total = inverse_ref[spot : spot + 1] * vectors[0]
                for j in range(1, i + 1):
                    total = total + inverse_ref[spot + j : spot + j + 1] * vectors[j]
                out_ref[i, 0, level, part] = total
                spot += i + 1
        return carry

    lax.fori_loop(0, depth, one_level, 0)


def on_device(gx_count, gy_count, start_vector, viscosity, friction, shifts):
    levels, rows, lanes = viscosity.shape
    count = shifts.shape[0] + 1
    wide = rows + 2 * HALO
    tiles = (count * (count + 1) // 2 + 7) // 8
    f32 = jnp.float32
    coef = pltpu.VMEM((2, levels, wide, lanes), f32)
    dma = pltpu.SemaphoreType.DMA
    vmem = pl.BlockSpec(memory_space=pltpu.VMEM)
    hbm = pl.BlockSpec(memory_space=pltpu.HBM)
    devices = gx_count * gy_count
    operands = [
        pltpu.with_memory_space_constraint(x, pltpu.HBM)
        for x in (start_vector, viscosity, friction, shifts)
    ]
    ortho_one, factor, inverse = pl.pallas_call(
        functools.partial(kernel, gx_count, gy_count),
        out_shape=(
            jax.ShapeDtypeStruct((count,) + start_vector.shape, f32),
            jax.ShapeDtypeStruct((count, count), f32),
            jax.ShapeDtypeStruct((8 * tiles, lanes), f32),
        ),
        in_specs=[hbm] * 4,
        out_specs=(vmem, vmem, vmem),
        scratch_shapes=[
            pltpu.VMEM(start_vector.shape, f32),
            pltpu.VMEM(viscosity.shape, f32),
            pltpu.VMEM(friction.shape, f32),
            pltpu.SMEM(shifts.shape, f32),
            dma((4,)),
            pltpu.VMEM((2, 2, 2, levels + 2, wide, lanes), f32),
            pltpu.VMEM((2, levels + 2, wide, lanes), f32),
            coef,
            coef,
            coef,
            coef,
            coef,
            coef,
            coef,
            coef,
            pltpu.VMEM((levels // 2, rows, lanes), f32),
            pltpu.VMEM((2, levels // 2, wide, lanes), f32),
            pltpu.VMEM((lanes, lanes), f32),
            pltpu.VMEM((2, 8, lanes), f32),
            pltpu.VMEM((2, devices, lanes), f32),
            pltpu.VMEM((8 * tiles, lanes), f32),
            dma((2, 3)),
            dma((2, 3)),
            dma((6,)),
            dma((6,)),
            dma((2,)),
            dma((2,)),
        ],
        compiler_params=pltpu.CompilerParams(
            collective_id=0, has_side_effects=True, vmem_limit_bytes=40 * 2**20
        ),
    )(*operands)
    depth = 8 if levels % 8 == 0 else 1
    block = pl.BlockSpec((count, 1, depth, rows, lanes), lambda c, z: (0, c, z, 0, 0))
    orthonormal, factor = pl.pallas_call(
        finish,
        grid=(2, levels // depth),
        out_shape=(
            jax.ShapeDtypeStruct(ortho_one.shape, f32),
            jax.ShapeDtypeStruct(factor.shape, f32),
        ),
        in_specs=[vmem, vmem, vmem],
        compiler_params=pltpu.CompilerParams(vmem_limit_bytes=12 * 2**20),
        out_specs=(block, pl.BlockSpec(factor.shape, lambda c, z: (0, 0))),
    )(inverse, ortho_one, factor)
    return orthonormal, factor


def solution(mesh):
    return jax.shard_map(
        functools.partial(on_device, mesh.shape["gx"], mesh.shape["gy"]),
        mesh=mesh,
        in_specs=(P(None, None, "gx", "gy"), P(None, "gx", "gy"), P(None, "gx", "gy"), P()),
        out_specs=(P(None, None, None, "gx", "gy"), P()),
        check_vma=False,
    )
```

```python
import functools

import jax
import jax.numpy as jnp
from jax import lax
from jax.experimental import pallas as pl
from jax.experimental.pallas import tpu as pltpu
from jax.sharding import PartitionSpec as P

MESH = pl.DeviceIdType.MESH
HALO = 8
GROUP = 2 * HALO
ETA, FRIC, BASIS = 0, 1, 2
CHUNK = 4
HALVES = (slice(0, 8), slice(8, 16))


def kernel(
    gx_count,
    gy_count,
    start_hbm,
    eta_hbm,
    fric_hbm,
    shift_hbm,
    out_ref,
    factor_ref,
    lower_inv,
    loaded,
    shift_ref,
    field,
    coef,
    own,
    beside,
    pack,
    pack_eta,
    pack_coef,
    red,
    mine,
    slots,
    splat,
    load_sem,
    row_send,
    row_recv,
    side_send,
    side_recv,
    gram_send,
    gram_recv,
):
    f32 = jnp.float32
    powers = shift_hbm.shape[0]
    count = powers + 1
    levels, rows, lanes = field.shape[2], field.shape[1] - 2 * HALO, field.shape[3]
    wide = rows + 2 * HALO
    places = wide // CHUNK
    me_x, me_y = lax.axis_index("gx"), lax.axis_index("gy")
    total_count = 2.0 * levels * rows * lanes * gx_count * gy_count
    devices = gx_count * gy_count
    me = me_x * gy_count + me_y

    def peer(step):
        other = lax.rem(me + step, devices)
        return (lax.div(other, gy_count), lax.rem(other, gy_count))

    loads = [
        pltpu.make_async_copy(src, dst, load_sem.at[n])
        for n, (src, dst) in enumerate(
            (
                (eta_hbm, loaded.at[ETA]),
                (fric_hbm, loaded.at[FRIC]),
                (start_hbm, loaded.at[pl.ds(BASIS, 2)]),
                (shift_hbm, shift_ref),
            )
        )
    ]
    for load in loads:
        load.start()
    barrier = pltpu.get_barrier_semaphore()
    for step in range(1, devices):
        pl.semaphore_signal(barrier, inc=1, device_id=peer(step), device_id_type=MESH)
    for load in loads:
        load.wait()

    lane = lax.broadcasted_iota(jnp.int32, (8, lanes), 1)
    level = lax.broadcasted_iota(jnp.int32, (8, lanes), 0)
    first, last = level == 0, level == 7
    in_group = lane % GROUP
    place_of = lane // GROUP

    for x in range(rows):
        for n in range(4):
            for h in range(2):
                field[n, HALO + x, HALVES[h]] = loaded[n, pl.ds(x + rows * h, 8, stride=2 * rows)]

    pl.semaphore_wait(barrier, devices - 1)

    up_ok, down_ok = me_x > 0, me_x < gx_count - 1
    left_ok, right_ok = me_y > 0, me_y < gy_count - 1
    row_ways = (
        (down_ok, jnp.minimum(me_x + 1, gx_count - 1), rows, 0),
        (up_ok, jnp.maximum(me_x - 1, 0), HALO, rows + HALO),
    )
    side_ways = (
        (right_ok, jnp.minimum(me_y + 1, gy_count - 1)),
        (left_ok, jnp.maximum(me_y - 1, 0)),
    )

    def row_copy(way, part):
        _, other, src, dst = row_ways[way]
        return pltpu.make_async_remote_copy(
            src_ref=field.at[pl.ds(2 * part, 2), pl.ds(src, HALO)],
            dst_ref=field.at[pl.ds(2 * part, 2), pl.ds(dst, HALO)],
            send_sem=row_send.at[way, part],
            recv_sem=row_recv.at[way, part],
            device_id=(other, me_y),
            device_id_type=MESH,
        )

    def side_copy(way):
        return pltpu.make_async_remote_copy(
            src_ref=own,
            dst_ref=beside.at[way],
            send_sem=side_send.at[way],
            recv_sem=side_recv.at[way],
            device_id=(me_x, side_ways[way][1]),
            device_id_type=MESH,
        )

    for part in range(2):
        for way in range(2):

            @pl.when(row_ways[way][0])
            def _():
                row_copy(way, part).start()

    def blank(ref, shape):
        ref[ETA] = jnp.zeros(shape, f32)
        ref[FRIC] = jnp.ones(shape, f32)
        for comp in range(2):
            ref[BASIS + comp] = jnp.zeros(shape, f32)

    for way in range(2):

        @pl.when(jnp.logical_not(row_ways[1 - way][0]))
        def _():
            blank(field.at[pl.ds(0, 4), pl.ds(row_ways[way][3], HALO)], (HALO, levels, lanes))

        @pl.when(jnp.logical_not(side_ways[1 - way][0]))
        def _():
            blank(beside.at[way], (CHUNK, levels, lanes))

    def turn(value, shift):
        return pltpu.roll(value, shift % lanes, 1)

    def smooth_levels(even, odd):
        pair = even + odd
        lower = even + jnp.where(first, 0.0, pltpu.roll(odd, 1, 0))
        upper = jnp.where(last, odd, pltpu.roll(lower, 7, 0))
        return pair + lower, pair + upper

    def pairs_of(values):
        return [[a[h] + b[h] for h in range(2)] for a, b in zip(values, values[1:])]

    def coefficients(etas, frics, gates):
        sums = pairs_of(etas)
        results = []
        for r in range(len(frics)):
            smooth = smooth_levels(*[sums[r][h] + sums[r + 1][h] for h in range(2)])
            parts = []
            for h in range(2):
                here, value = etas[r + 1][h], smooth[h]
                around = (value + value) + (turn(value, 1) + turn(value, -1))
                diagonal = frics[r][h] + 6.0 * here + 0.125 * around
                g = (0.125 * gates[r]) / diagonal
                a = here * g
                parts.append(
                    (1.0 + 16.0 * a, a + a, g + g, turn(a, 1), turn(g, 1), turn(a, -1), turn(g, -1))
                )
            results.append(parts)
        return results

    def stencil(values, etas, coefs, newton):
        size = len(coefs)
        sums = [pairs_of(values[c]) for c in range(2)]
        scaled = [
            pairs_of([[e[h] * v[h] for h in range(2)] for e, v in zip(etas, values[c])])
            for c in range(2)
        ]
        results = [[None] * size for _ in range(2)]
        for r in range(size):
            crossed = []
            for c in range(2):
                slope = [sums[c][r + 1][h] - sums[c][r][h] for h in range(2)]
                crossed.append([d + d for d in slope])
            for c in range(2):
                plain = smooth_levels(*[sums[c][r][h] + sums[c][r + 1][h] for h in range(2)])
                weighted = smooth_levels(*[scaled[c][r][h] + scaled[c][r + 1][h] for h in range(2)])
                out = []
                for h in range(2):
                    centre_c, a_mid, g_mid, a_up, g_up, a_down, g_down = coefs[r](h)
                    p, q, cross = plain[h], weighted[h], crossed[1 - c][h]
                    centre = (centre_c - newton) * values[c][r + 1][h] - (a_mid * p + g_mid * q)
                    ups = a_up * (p - cross) + g_up * q
                    downs = a_down * (p + cross) + g_down * q
                    out.append(centre - (turn(ups, -1) + turn(downs, 1)))
                results[c][r] = out
        return results

    def row_of(ref, n, x):
        return [ref[n, x, half] for half in HALVES]

    def row_coefficients(start, size):
        etas = [row_of(field, ETA, start - 1 + r) for r in range(size + 2)]
        frics = [row_of(field, FRIC, start + r) for r in range(size)]
        gates = []
        for r in range(size):
            x = start + r
            inside = ((x >= HALO) | up_ok) & ((x < rows + HALO) | down_ok)
            gates.append(jnp.where(inside, 1.0, 0.0))
        for r, parts in enumerate(coefficients(etas, frics, gates)):
            for h in range(2):
                for n in range(7):
                    coef[n, start + r, HALVES[h]] = parts[h][n]

    def main_chunk(power, start):
        newton = shift_ref[power - 1]
        before = BASIS + 2 * (power - 1)
        values = [
            [row_of(field, before + c, start - 1 + r) for r in range(CHUNK + 2)] for c in range(2)
        ]
        etas = [row_of(field, ETA, start - 1 + r) for r in range(CHUNK + 2)]
        coefs = [
            lambda h, r=r: [coef[n, start + r, HALVES[h]] for n in range(7)] for r in range(CHUNK)
        ]
        results = stencil(values, etas, coefs, newton)
        for c in range(2):
            for r in range(CHUNK):
                for h in range(2):
                    field[before + 2 + c, start + r, HALVES[h]] = results[c][r][h]

    def span(power, low, high):
        def one(n, carry):
            main_chunk(power, jnp.minimum(low + CHUNK * n, high - CHUNK))
            return carry

        lax.fori_loop(0, lax.div(high - low + CHUNK - 1, CHUNK), one, 0)

    def put_own(n, g_range, fresh):
        for s in range(CHUNK):
            for half in HALVES:
                tile = jnp.zeros((8, lanes), f32) if fresh else own[n, s, half]
                for g in g_range:
                    turned = turn(field[n, CHUNK * g + s, half], GROUP * g + HALO)
                    tile = jnp.where(place_of == g, turned, tile)
                own[n, s, half] = tile

    inner_places = range(HALO // CHUNK, (HALO + rows) // CHUNK)
    outer_places = [g for g in range(places) if g not in inner_places]

    def own_inner(n, carry):
        put_own(n, inner_places, True)
        return carry

    def own_outer(n, carry):
        put_own(n, outer_places, False)
        return carry

    lax.fori_loop(0, 4, own_inner, 0)

    def inner_rows(n, carry):
        row_coefficients(HALO + 1 + n * (rows - 2 - HALO), HALO)
        return carry

    def outer_rows(n, carry):
        row_coefficients(1 + n * (rows + HALO - 2), HALO)
        return carry

    lax.fori_loop(0, 2, inner_rows, 0)

    half_way = powers // 2

    def inner_power(power, carry):
        span(power, HALO + power, HALO + rows - power)
        return carry

    lax.fori_loop(1, half_way + 1, inner_power, 0)

    for part in range(2):
        for way in range(2):

            @pl.when(row_ways[1 - way][0])
            def _():
                row_copy(way, part).wait_recv()

    lax.fori_loop(0, 4, own_outer, 0)
    for way in range(2):

        @pl.when(side_ways[way][0])
        def _():
            side_copy(way).start()

    lax.fori_loop(0, 2, outer_rows, 0)

    def outer_power(power, carry):
        def one(n, inner_carry):
            skip = lax.div(n, 2) * (rows - 2 * power)
            main_chunk(power, power + CHUNK * n + skip)
            return inner_carry

        return lax.fori_loop(0, 4, one, carry)

    lax.fori_loop(1, half_way + 1, outer_power, 0)

    for way in range(2):

        @pl.when(side_ways[1 - way][0])
        def _():
            side_copy(way).wait_recv()

    row_inside = ((place_of >= HALO // CHUNK) | up_ok) & (
        (place_of < (HALO + rows) // CHUNK) | down_ok
    )
    side_inside = (row_inside & ((in_group >= HALO) | left_ok), row_inside & ((in_group < HALO) | right_ok))
    own_part = (in_group >= HALO, in_group < HALO)

    def wrapped(values):
        return (
            [[turn(v, GROUP) for v in values[-1]]]
            + values
            + [[turn(v, -GROUP) for v in values[0]]]
        )

    for side in range(2):
        fields = [
            [
                [
                    jnp.where(own_part[side], own[n, s, half], beside[side, n, s, half])
                    for half in HALVES
                ]
                for s in range(CHUNK)
            ]
            for n in range(4)
        ]
        etas = wrapped(fields[ETA])
        gate = jnp.where(side_inside[side], 1.0, 0.0)
        for r, parts in enumerate(coefficients(etas, fields[FRIC], [gate] * CHUNK)):
            for h in range(2):
                for n in range(7):
                    pack_coef[n, side, r, HALVES[h]] = parts[h][n]
        for r in range(CHUNK + 2):
            for h in range(2):
                pack_eta[side, r, HALVES[h]] = etas[r][h]
        for c in range(2):
            for r, value in enumerate(wrapped(fields[BASIS + c])):
                for h in range(2):
                    pack[0, side, c, r, HALVES[h]] = value[h]

    edge = (lane < HALO // 2) | (lane >= lanes - HALO // 2)

    def merge(power, both, places_now):
        for c in range(2):
            for s in range(CHUNK):
                for h in range(2):
                    mixed = jnp.where(own_part[0], both[0][c][s][h], both[1][c][s][h])
                    for g in places_now:
                        x = CHUNK * g + s
                        turned = turn(mixed, -(GROUP * g + HALO))
                        spot = BASIS + 2 * power + c
                        field[spot, x, HALVES[h]] = jnp.where(
                            edge, turned, field[spot, x, HALVES[h]]
                        )

    def pack_power(power):
        newton = shift_ref[power - 1]
        now, later = lax.rem(power - 1, 2), lax.rem(power, 2)
        both = []
        for side in range(2):
            values = [
                [[pack[now, side, c, r, half] for half in HALVES] for r in range(CHUNK + 2)]
                for c in range(2)
            ]
            etas = [[pack_eta[side, r, half] for half in HALVES] for r in range(CHUNK + 2)]
            coefs = [
                lambda h, r=r: [pack_coef[n, side, r, HALVES[h]] for n in range(7)]
                for r in range(CHUNK)
            ]
            results = stencil(values, etas, coefs, newton)
            both.append(results)
            for c in range(2):
                for r, value in enumerate(wrapped(results[c])):
                    for h in range(2):
                        pack[later, side, c, r, HALVES[h]] = value[h]
        merge(power, both, inner_places)

    def early_pack(power, carry):
        pack_power(power)
        return carry

    lax.fori_loop(1, half_way + 1, early_pack, 0)

    spot = half_way % 2
    near = (in_group >= HALO + half_way, in_group < HALO - half_way)
    resync_places = range(half_way // CHUNK, (wide - half_way) // CHUNK)
    before_sync = [
        [
            [[pack[spot, side, c, 1 + s, half] for half in HALVES] for s in range(CHUNK)]
            for c in range(2)
        ]
        for side in range(2)
    ]
    for c in range(2):
        for s in range(CHUNK):
            for h in range(2):
                tile = jnp.zeros((8, lanes), f32)
                for g in resync_places:
                    turned = turn(
                        field[BASIS + 2 * half_way + c, CHUNK * g + s, HALVES[h]], GROUP * g + HALO
                    )
                    tile = jnp.where(place_of == g, turned, tile)
                for side in range(2):
                    value = jnp.where(near[side], tile, before_sync[side][c][s][h])
                    pack[spot, side, c, 1 + s, HALVES[h]] = value
                    if s == CHUNK - 1:
                        pack[spot, side, c, 0, HALVES[h]] = turn(value, GROUP)
                    if s == 0:
                        pack[spot, side, c, CHUNK + 1, HALVES[h]] = turn(value, -GROUP)
    merge(half_way, before_sync, [g for g in resync_places if g not in inner_places])

    def late_power(power, carry):
        span(power, power, wide - power)
        pack_power(power)
        return carry

    lax.fori_loop(half_way + 1, powers + 1, late_power, 0)

    pairs = [(i, j) for i in range(count) for j in range(i + 1)]
    place = {pair: n for n, pair in enumerate(pairs)}
    padded = red.shape[0]
    red[...] = jnp.zeros((padded, lanes), jnp.float32)
    ones = jnp.ones((8, lanes), jnp.float32)
    splat_rows = splat.shape[0]
    diagonal = lax.broadcasted_iota(jnp.int32, (splat_rows, lanes), 1) == lax.broadcasted_iota(
        jnp.int32, (splat_rows, lanes), 0
    )

    def add_products(sums, vectors):
        return tuple(total + vectors[i] * vectors[j] for total, (i, j) in zip(sums, pairs))

    zeros = tuple(jnp.zeros((8, lanes), jnp.float32) for _ in pairs)

    def gram_of(sums, phase):
        for n, total in enumerate(sums):
            red[n : n + 1] = jnp.sum(total, axis=0, keepdims=True)
        mine[phase] = lax.dot_general(
            ones,
            red[...],
            (((1,), (1,)), ((), ())),
            precision=lax.Precision.HIGHEST,
            preferred_element_type=jnp.float32,
        )
        for step in range(1, devices):
            pltpu.make_async_remote_copy(
                src_ref=mine.at[phase, pl.ds(0, 1)],
                dst_ref=slots.at[phase, pl.ds(me, 1)],
                send_sem=gram_send.at[phase],
                recv_sem=gram_recv.at[phase],
                device_id=peer(step),
                device_id_type=MESH,
            ).start()
        slots[phase, pl.ds(me, 1)] = mine[phase, 0:1]
        every = pltpu.make_async_remote_copy(
            src_ref=slots.at[phase, pl.ds(0, devices - 1)],
            dst_ref=slots.at[phase, pl.ds(0, devices - 1)],
            send_sem=gram_send.at[phase],
            recv_sem=gram_recv.at[phase],
            device_id=peer(1),
            device_id_type=MESH,
        )
        every.wait_recv()
        whole = jnp.sum(slots[phase], axis=0, keepdims=True) / total_count
        spread = jnp.where(diagonal, jnp.broadcast_to(whole, diagonal.shape), 0.0)
        splat[...] = jnp.broadcast_to(jnp.sum(spread, axis=1, keepdims=True), spread.shape)
        every.wait_send()
        return {pair: splat[n : n + 1] for n, pair in enumerate(pairs)}

    def factorise(gram):
        left = dict(gram)
        low, inv = {}, {}
        for j in range(count):
            root = jnp.sqrt(left[j, j])
            scale = 1.0 / root
            low[j, j], inv[j, j] = root, scale
            for i in range(j + 1, count):
                low[i, j] = left[i, j] * scale
            for i in range(j + 1, count):
                for k in range(j + 1, i + 1):
                    left[i, k] = left[i, k] - low[i, j] * low[k, j]
        for i in range(count):
            for j in range(i):
                total = low[i, j] * inv[j, j]
                for k in range(j + 1, i):
                    total = total + low[i, k] * inv[k, j]
                inv[i, j] = -(total * inv[i, i])
        for pair, n in place.items():
            lower_inv[n : n + 1] = inv[pair]
        return low

    def combine(vectors):
        results = []
        for i in range(count):
            total = lower_inv[place[i, 0] : place[i, 0] + 1] * vectors[0]
            for j in range(1, i + 1):
                total = total + lower_inv[place[i, j] : place[i, j] + 1] * vectors[j]
            results.append(total)
        return results

    def basis_at(spot, half):
        comp, x = lax.div(spot, rows), lax.rem(spot, rows)
        return [field[BASIS + 2 * n + comp, HALO + x, HALVES[half]] for n in range(count)]

    def gram_step(spot, sums):
        for half in range(2):
            sums = add_products(sums, basis_at(spot, half))
        return sums

    low_one = factorise(gram_of(lax.fori_loop(0, 2 * rows, gram_step, zeros), 0))

    def ortho_step(spot, sums):
        comp, x = lax.div(spot, rows), lax.rem(spot, rows)
        for half in range(2):
            vectors = combine(basis_at(spot, half))
            for n in range(count):
                out_ref[n, comp, x, HALVES[half]] = vectors[n]
            sums = add_products(sums, vectors)
        return sums

    low_two = factorise(gram_of(lax.fori_loop(0, 2 * rows, ortho_step, zeros), 1))

    fac_row = lax.broadcasted_iota(jnp.int32, (count, count), 0)
    fac_col = lax.broadcasted_iota(jnp.int32, (count, count), 1)
    factor = jnp.zeros((count, count), jnp.float32)
    for i in range(count):
        for j in range(i, count):
            total = low_two[i, i] * low_one[j, i]
            for k in range(i + 1, j + 1):
                total = total + low_two[k, i] * low_one[j, k]
            factor = jnp.where((fac_row == i) & (fac_col == j), total[:, :count], factor)
    factor_ref[...] = factor

    for way in range(2):

        @pl.when(row_ways[way][0])
        def _():
            for part in range(2):
                row_copy(way, part).wait_send()

        @pl.when(side_ways[way][0])
        def _():
            side_copy(way).wait_send()


def finish(inverse_ref, basis_ref, factor_in, out_ref, factor_ref):
    count, _, depth, rows, _ = out_ref.shape
    levels = basis_ref.shape[2] // rows
    comp, low = pl.program_id(0), pl.program_id(1) * depth
    factor_ref[...] = factor_in[...]

    def one_level(n, carry):
        spot_row = lax.div(low + n, 2) + 8 * lax.rem(low + n, 2)
        for half in range(rows // 8):
            part = slice(8 * half, 8 * half + 8)
            vectors = [
                basis_ref[n_basis, comp, pl.ds(8 * levels * half + spot_row, 8, stride=levels)]
                for n_basis in range(count)
            ]
            spot = 0
            for i in range(count):
                total = inverse_ref[spot : spot + 1] * vectors[0]
                for j in range(1, i + 1):
                    total = total + inverse_ref[spot + j : spot + j + 1] * vectors[j]
                out_ref[i, 0, n, part] = total
                spot += i + 1
        return carry

    lax.fori_loop(0, depth, one_level, 0)


def on_device(gx_count, gy_count, start_vector, viscosity, friction, shifts):
    levels, rows, lanes = viscosity.shape
    count = shifts.shape[0] + 1
    wide = rows + 2 * HALO
    tiles = (count * (count + 1) // 2 + 7) // 8
    f32 = jnp.float32
    dma = pltpu.SemaphoreType.DMA
    vmem = pl.BlockSpec(memory_space=pltpu.VMEM)
    hbm = pl.BlockSpec(memory_space=pltpu.HBM)
    devices = gx_count * gy_count
    flat = (levels * rows, lanes)
    operands = [
        pltpu.with_memory_space_constraint(x, pltpu.HBM)
        for x in (
            start_vector.reshape((2,) + flat),
            viscosity.reshape(flat),
            friction.reshape(flat),
            shifts,
        )
    ]
    ortho_one, factor, inverse = pl.pallas_call(
        functools.partial(kernel, gx_count, gy_count),
        out_shape=(
            jax.ShapeDtypeStruct((count, 2, rows, levels, lanes), f32),
            jax.ShapeDtypeStruct((count, count), f32),
            jax.ShapeDtypeStruct((8 * tiles, lanes), f32),
        ),
        in_specs=[hbm] * 4,
        out_specs=(vmem, vmem, vmem),
        scratch_shapes=[
            pltpu.VMEM((4,) + flat, f32),
            pltpu.SMEM(shifts.shape, f32),
            pltpu.VMEM((BASIS + 2 * count, wide, levels, lanes), f32),
            pltpu.VMEM((7, wide, levels, lanes), f32),
            pltpu.VMEM((4, CHUNK, levels, lanes), f32),
            pltpu.VMEM((2, 4, CHUNK, levels, lanes), f32),
            pltpu.VMEM((2, 2, 2, CHUNK + 2, levels, lanes), f32),
            pltpu.VMEM((2, CHUNK + 2, levels, lanes), f32),
            pltpu.VMEM((7, 2, CHUNK, levels, lanes), f32),
            pltpu.VMEM((lanes, lanes), f32),
            pltpu.VMEM((2, 8, lanes), f32),
            pltpu.VMEM((2, devices, lanes), f32),
            pltpu.VMEM((8 * tiles, lanes), f32),
            dma((4,)),
            dma((2, 2)),
            dma((2, 2)),
            dma((2,)),
            dma((2,)),
            dma((2,)),
            dma((2,)),
        ],
        compiler_params=pltpu.CompilerParams(
            collective_id=0, has_side_effects=True, vmem_limit_bytes=40 * 2**20
        ),
    )(*operands)
    depth = 8 if levels % 8 == 0 else 1
    block = pl.BlockSpec((count, 1, depth, rows, lanes), lambda c, z: (0, c, z, 0, 0))
    return tuple(
        pl.pallas_call(
            finish,
            grid=(2, levels // depth),
            out_shape=(
                jax.ShapeDtypeStruct((count,) + start_vector.shape, f32),
                jax.ShapeDtypeStruct(factor.shape, f32),
            ),
            in_specs=[vmem, vmem, vmem],
            compiler_params=pltpu.CompilerParams(vmem_limit_bytes=12 * 2**20),
            out_specs=(block, pl.BlockSpec(factor.shape, lambda c, z: (0, 0))),
        )(inverse, ortho_one.reshape(count, 2, rows * levels, lanes), factor)
    )


def solution(mesh):
    return jax.shard_map(
        functools.partial(on_device, mesh.shape["gx"], mesh.shape["gy"]),
        mesh=mesh,
        in_specs=(P(None, None, "gx", "gy"), P(None, "gx", "gy"), P(None, "gx", "gy"), P()),
        out_specs=(P(None, None, None, "gx", "gy"), P()),
        check_vma=False,
    )
```

```python
import functools

import jax
import jax.numpy as jnp
from jax import lax
from jax.experimental import pallas as pl
from jax.experimental.pallas import tpu as pltpu
from jax.sharding import PartitionSpec as P

MESH = pl.DeviceIdType.MESH
HALO = 8
GROUP = 2 * HALO
ETA, FRIC, BASIS = 0, 1, 2
CHUNK = 4
NEAR = 4
HALVES = (slice(0, 8), slice(8, 16))


def kernel(
    gx_count,
    gy_count,
    start_hbm,
    eta_hbm,
    fric_hbm,
    shift_hbm,
    out_ref,
    factor_ref,
    lower_inv,
    loaded,
    shift_ref,
    field,
    coef,
    own,
    side_own,
    corner_own,
    beside,
    corner,
    mixed,
    sync,
    pack,
    pack_eta,
    pack_coef,
    red,
    mine,
    slots,
    splat,
    load_sem,
    row_send,
    row_recv,
    side_send,
    side_recv,
    corner_send,
    corner_recv,
    gram_send,
    gram_recv,
):
    f32 = jnp.float32
    powers = shift_hbm.shape[0]
    count = powers + 1
    levels, rows, lanes = field.shape[2], field.shape[1] - 2 * HALO, field.shape[3]
    wide = rows + 2 * HALO
    places = wide // CHUNK
    me_x, me_y = lax.axis_index("gx"), lax.axis_index("gy")
    total_count = 2.0 * levels * rows * lanes * gx_count * gy_count
    devices = gx_count * gy_count
    me = me_x * gy_count + me_y

    def peer(step):
        other = lax.rem(me + step, devices)
        return (lax.div(other, gy_count), lax.rem(other, gy_count))

    loads = [
        pltpu.make_async_copy(src, dst, load_sem.at[n])
        for n, (src, dst) in enumerate(
            (
                (shift_hbm, shift_ref),
                *((eta_hbm.at[:, h], loaded.at[ETA, h]) for h in range(2)),
                *((fric_hbm.at[:, h], loaded.at[FRIC, h]) for h in range(2)),
                *(
                    (start_hbm.at[c, :, h], loaded.at[BASIS + c, h])
                    for c in range(2)
                    for h in range(2)
                ),
            )
        )
    ]
    for load in loads:
        load.start()
    barrier = pltpu.get_barrier_semaphore()
    for step in range(1, devices):
        pl.semaphore_signal(barrier, inc=1, device_id=peer(step), device_id_type=MESH)
    for load in loads:
        load.wait()

    lane = lax.broadcasted_iota(jnp.int32, (8, lanes), 1)
    level = lax.broadcasted_iota(jnp.int32, (8, lanes), 0)
    first, last = level == 0, level == 7
    in_group = lane % GROUP
    place_of = lane // GROUP

    flat = loaded.reshape(4, 2, 8 * rows, lanes)
    for x in range(rows):
        for n in range(4):
            for h in range(2):
                field[n, HALO + x, HALVES[h]] = flat[n, h, pl.ds(x, 8, stride=rows)]

    def turn(value, shift):
        return pltpu.roll(value, shift % lanes, 1)

    def gather(n, spots, tile):
        for half in range(2):
            tiles = tile[half]
            for g, x in spots:
                turned = turn(field[n, x, HALVES[half]], GROUP * g + HALO)
                tiles = jnp.where(place_of == g, turned, tiles)
            yield tiles

    empty = [jnp.zeros((8, lanes), f32)] * 2
    inner_places = range(HALO // CHUNK, (HALO + rows) // CHUNK)
    outer_places = [g for g in range(places) if g not in inner_places]
    folded = {}
    for n in range(4):
        for s in range(CHUNK):
            spots = [(g, CHUNK * g + s) for g in inner_places]
            for half, tile in enumerate(gather(n, spots, empty)):
                own[n, s, HALVES[half]] = tile
        for way in range(2):
            first_row = (rows, HALO)[way]
            spots = [
                (2 * s + k, first_row + CHUNK * k + s) for s in range(CHUNK) for k in range(2)
            ]
            for half, tile in enumerate(gather(n, spots, empty)):
                folded[way, n, half] = tile

    upper_lanes = in_group >= HALO
    inner_lanes = (place_of >= inner_places[0]) & (place_of <= inner_places[-1])
    for n in range(4):
        for half in HALVES:
            two = [
                jnp.where(inner_lanes, own[n, 2 * k, half], turn(own[n, 2 * k + 1, half], lanes // 2))
                for k in range(2)
            ]
            side_own[0, n, half] = jnp.where(upper_lanes, turn(two[1], HALO), two[0])
            side_own[1, n, half] = jnp.where(upper_lanes, two[0], turn(two[1], -HALO))
        for way in range(2):
            one, other = folded[way, n, 0], folded[way, n, 1]
            corner_own[0, way, n] = jnp.where(upper_lanes, turn(other, HALO), one)
            corner_own[1, way, n] = jnp.where(upper_lanes, one, turn(other, -HALO))

    pl.semaphore_wait(barrier, devices - 1)

    up_ok, down_ok = me_x > 0, me_x < gx_count - 1
    left_ok, right_ok = me_y > 0, me_y < gy_count - 1
    row_ways = (
        (down_ok, jnp.minimum(me_x + 1, gx_count - 1), (rows + NEAR, rows), (NEAR, 0)),
        (
            up_ok,
            jnp.maximum(me_x - 1, 0),
            (HALO, HALO + NEAR),
            (HALO + rows, HALO + rows + NEAR),
        ),
    )
    side_ways = (
        (right_ok, jnp.minimum(me_y + 1, gy_count - 1)),
        (left_ok, jnp.maximum(me_y - 1, 0)),
    )

    def row_copy(way, part):
        _, other, src, dst = row_ways[way]
        return pltpu.make_async_remote_copy(
            src_ref=field.at[pl.ds(0, 4), pl.ds(src[part], NEAR)],
            dst_ref=field.at[pl.ds(0, 4), pl.ds(dst[part], NEAR)],
            send_sem=row_send.at[way, part],
            recv_sem=row_recv.at[way, part],
            device_id=(other, me_y),
            device_id_type=MESH,
        )

    def corner_copy(way, side):
        return pltpu.make_async_remote_copy(
            src_ref=corner_own.at[side, way],
            dst_ref=corner.at[side, way],
            send_sem=corner_send.at[side, way],
            recv_sem=corner_recv.at[side, way],
            device_id=(row_ways[way][1], side_ways[side][1]),
            device_id_type=MESH,
        )

    def corner_goes(way, side):
        return row_ways[way][0] & side_ways[side][0]

    corners = [(way, side) for way in range(2) for side in range(2)]

    def side_copy(way):
        return pltpu.make_async_remote_copy(
            src_ref=side_own.at[way],
            dst_ref=beside.at[way],
            send_sem=side_send.at[way],
            recv_sem=side_recv.at[way],
            device_id=(me_x, side_ways[way][1]),
            device_id_type=MESH,
        )

    for part in range(2):
        for way in range(2):

            @pl.when(row_ways[way][0])
            def _():
                row_copy(way, part).start()

    for way in range(2):

        @pl.when(side_ways[way][0])
        def _():
            side_copy(way).start()

    for way, side in corners:

        @pl.when(corner_goes(way, side))
        def _():
            corner_copy(way, side).start()

    def blank(ref, shape):
        ref[ETA] = jnp.zeros(shape, f32)
        ref[FRIC] = jnp.ones(shape, f32)
        for comp in range(2):
            ref[BASIS + comp] = jnp.zeros(shape, f32)

    for way in range(2):

        @pl.when(jnp.logical_not(row_ways[1 - way][0]))
        def _():
            blank(
                field.at[pl.ds(0, 4), pl.ds(min(row_ways[way][3]), HALO)], (HALO, levels, lanes)
            )

        @pl.when(jnp.logical_not(side_ways[1 - way][0]))
        def _():
            blank(beside.at[way], (levels, lanes))

    for way, side in corners:

        @pl.when(jnp.logical_not(corner_goes(1 - way, 1 - side)))
        def _():
            blank(corner.at[side, way], (8, lanes))

    def smooth_levels(even, odd):
        pair = even + odd
        lower = even + jnp.where(first, 0.0, pltpu.roll(odd, 1, 0))
        upper = jnp.where(last, odd, pltpu.roll(lower, 7, 0))
        return pair + lower, pair + upper

    def pairs_of(values):
        return [[a[h] + b[h] for h in range(2)] for a, b in zip(values, values[1:])]

    def coefficients(etas, frics, gates):
        sums = pairs_of(etas)
        results = []
        for r in range(len(frics)):
            smooth = smooth_levels(*[sums[r][h] + sums[r + 1][h] for h in range(2)])
            parts = []
            for h in range(2):
                here, value = etas[r + 1][h], smooth[h]
                around = (value + value) + (turn(value, 1) + turn(value, -1))
                diagonal = frics[r][h] + 6.0 * here + 0.125 * around
                g = (0.125 * gates[r]) / diagonal
                a = here * g
                parts.append(
                    (1.0 + 16.0 * a, a + a, g + g, turn(a, 1), turn(g, 1), turn(a, -1), turn(g, -1))
                )
            results.append(parts)
        return results

    def stream(newton, value, eta, coefs, low, high, store, lag=2):
        def load(r):
            e = eta(r)
            values = [value(c, r) for c in range(2)]
            return values, [[e[h] * v[h] for h in range(2)] for v in values]

        def add(one, two):
            return [[[one[k][c][h] + two[k][c][h] for h in range(2)] for c in range(2)] for k in range(2)]

        def finish_row(r, parts):
            for c in range(2):
                store(c, r, [centre - (up + down) for centre, up, down in parts[c]])

        here = load(low)
        pair = add(load(low - 1), here)
        pending = []
        for r in range(low, high):
            after = load(r + 1)
            next_pair = add(here, after)
            crossed = []
            for c in range(2):
                slope = [next_pair[0][c][h] - pair[0][c][h] for h in range(2)]
                crossed.append([d + d for d in slope])
            parts = []
            for c in range(2):
                plain, weighted = [
                    smooth_levels(*[pair[k][c][h] + next_pair[k][c][h] for h in range(2)])
                    for k in range(2)
                ]
                out = []
                for h in range(2):
                    centre_c, a_mid, g_mid, a_up, g_up, a_down, g_down = coefs(r, h)
                    p, q, cross = plain[h], weighted[h], crossed[1 - c][h]
                    ups = a_up * (p - cross) + g_up * q
                    downs = a_down * (p + cross) + g_down * q
                    up, down = turn(ups, -1), turn(downs, 1)
                    centre = (centre_c - newton) * here[0][c][h] - (a_mid * p + g_mid * q)
                    out.append((centre, up, down))
                parts.append(out)
            pending.append((r, parts))
            if len(pending) > lag:
                finish_row(*pending.pop(0))
            here, pair = after, next_pair
        for r, parts in pending:
            finish_row(r, parts)

    def row_of(ref, n, x):
        return [ref[n, x, half] for half in HALVES]

    def row_coefficients(start, size):
        etas = [row_of(field, ETA, start - 1 + r) for r in range(size + 2)]
        frics = [row_of(field, FRIC, start + r) for r in range(size)]
        gates = []
        for r in range(size):
            x = start + r
            inside = ((x >= HALO) | up_ok) & ((x < rows + HALO) | down_ok)
            gates.append(jnp.where(inside, 1.0, 0.0))
        for r, parts in enumerate(coefficients(etas, frics, gates)):
            for h in range(2):
                for n in range(7):
                    coef[n, start + r, HALVES[h]] = parts[h][n]

    def merged(c, r, h, value):
        turned = turn(mixed[c, r % CHUNK, HALVES[h]], -(GROUP * (r // CHUNK) + HALO))
        return jnp.where(edge, turned, value)

    def main_rows(power, low, high, merging=False):
        before = BASIS + 2 * (power - 1)

        def store(c, r, out):
            for h in range(2):
                result = out[h]
                if merging and HALO <= r < HALO + rows:
                    result = merged(c, r, h, result)
                field[before + 2 + c, r, HALVES[h]] = result

        stream(
            shift_ref[power - 1],
            lambda c, r: row_of(field, before + c, r),
            lambda r: row_of(field, ETA, r),
            lambda r, h: [coef[n, r, HALVES[h]] for n in range(7)],
            low,
            high,
            store,
        )

    def merge(power, low, high):
        for c in range(2):
            for r in range(low, high):
                for h in range(2):
                    spot = BASIS + 2 * power + c
                    field[spot, r, HALVES[h]] = merged(c, r, h, field[spot, r, HALVES[h]])

    row_coefficients(HALO + 1, rows - 2)

    half_way = powers // 2
    edge = (lane < HALO // 2) | (lane >= lanes - HALO // 2)
    for power in range(1, half_way + 1):
        main_rows(power, HALO + power, HALO + rows - power)

    for part in range(2):
        for way in range(2):

            @pl.when(row_ways[1 - way][0])
            def _():
                row_copy(way, part).wait_recv()

        top = (NEAR, 0)[part]
        bottom = rows + 2 * HALO - NEAR - top
        row_coefficients(top + 1, NEAR)
        row_coefficients(bottom - 1, NEAR)
        for power in range(1, half_way + 1):
            main_rows(power, top + power, top + power + NEAR)
            main_rows(power, bottom - power, bottom - power + NEAR)

    for way in range(2):

        @pl.when(side_ways[1 - way][0])
        def _():
            side_copy(way).wait_recv()

    for way, side in corners:

        @pl.when(corner_goes(1 - way, 1 - side))
        def _():
            corner_copy(way, side).wait_recv()

    row_inside = ((place_of >= HALO // CHUNK) | up_ok) & (
        (place_of < (HALO + rows) // CHUNK) | down_ok
    )
    side_inside = (row_inside & ((in_group >= HALO) | left_ok), row_inside & ((in_group < HALO) | right_ok))
    own_part = (in_group >= HALO, in_group < HALO)

    def wrapped(values):
        return (
            [[turn(v, GROUP) for v in values[-1]]]
            + values
            + [[turn(v, -GROUP) for v in values[0]]]
        )

    own_rows = [
        [
            list(
                gather(
                    n, [(g, CHUNK * g + s) for g in outer_places], [own[n, s, half] for half in HALVES]
                )
            )
            for s in range(CHUNK)
        ]
        for n in range(4)
    ]

    def beside_rows(side, n, s, h):
        back = HALO if side else -HALO
        value = turn(beside[side, n, HALVES[h]], (s % 2) * (lanes // 2) + (s // 2) * back)
        for way in range(2):
            place = (0, places - HALO // CHUNK)[way]
            turned = turn(corner[side, way, n], GROUP * (place - 2 * s) + h * back)
            here = (place_of >= place) & (place_of < place + HALO // CHUNK)
            value = jnp.where(here, turned, value)
        return value

    for side in range(2):
        fields = [
            [
                [
                    jnp.where(
                        own_part[side], own_rows[n][s][h], beside_rows(side, n, s, h)
                    )
                    for h in range(2)
                ]
                for s in range(CHUNK)
            ]
            for n in range(4)
        ]
        etas = wrapped(fields[ETA])
        gate = jnp.where(side_inside[side], 1.0, 0.0)
        for r, parts in enumerate(coefficients(etas, fields[FRIC], [gate] * CHUNK)):
            for h in range(2):
                for n in range(7):
                    pack_coef[n, side, r, HALVES[h]] = parts[h][n]
        for r in range(CHUNK + 2):
            for h in range(2):
                pack_eta[side, r, HALVES[h]] = etas[r][h]
        for c in range(2):
            for r, value in enumerate(wrapped(fields[BASIS + c])):
                for h in range(2):
                    pack[0, side, c, r, HALVES[h]] = value[h]

    near = (in_group >= HALO + half_way, in_group < HALO - half_way)

    def pack_power(power):
        now, later = (power - 1) % 2, power % 2
        results = {}
        for side in range(2):

            def store(c, r, out):
                for h in range(2):
                    result = out[h]
                    results[side, c, r, h] = result
                    if side == 1:
                        mixed[c, r - 1, HALVES[h]] = jnp.where(
                            own_part[0], results[0, c, r, h], result
                        )
                    if power == half_way:
                        result = jnp.where(near[side], sync[c, r - 1, HALVES[h]], result)
                    pack[later, side, c, r, HALVES[h]] = result
                    if r == CHUNK:
                        pack[later, side, c, 0, HALVES[h]] = turn(result, GROUP)
                    if r == 1:
                        pack[later, side, c, CHUNK + 1, HALVES[h]] = turn(result, -GROUP)

            stream(
                shift_ref[power - 1],
                lambda c, r: [pack[now, side, c, r, half] for half in HALVES],
                lambda r: [pack_eta[side, r, half] for half in HALVES],
                lambda r, h: [pack_coef[n, side, r - 1, HALVES[h]] for n in range(7)],
                1,
                CHUNK + 1,
                store,
            )

    def make_sync():
        for c in range(2):
            for s in range(CHUNK):
                for half in HALVES:
                    tile = jnp.zeros((8, lanes), f32)
                    for g in range(half_way // CHUNK, (wide - half_way) // CHUNK):
                        turned = turn(
                            field[BASIS + 2 * half_way + c, CHUNK * g + s, half], GROUP * g + HALO
                        )
                        tile = jnp.where(place_of == g, turned, tile)
                    sync[c, s, half] = tile

    for power in range(1, half_way):
        pack_power(power)
        if power == half_way - 1:
            make_sync()
        merge(power, HALO, HALO + rows)
    pack_power(half_way)
    merge(half_way, half_way, wide - half_way)
    for power in range(half_way + 1, powers + 1):
        pack_power(power)
        main_rows(power, power, wide - power, True)

    pairs = [(i, j) for i in range(count) for j in range(i + 1)]
    place = {pair: n for n, pair in enumerate(pairs)}
    padded = red.shape[0]
    red[...] = jnp.zeros((padded, lanes), jnp.float32)
    ones = jnp.ones((8, lanes), jnp.float32)
    splat_rows = splat.shape[0]
    diagonal = lax.broadcasted_iota(jnp.int32, (splat_rows, lanes), 1) == lax.broadcasted_iota(
        jnp.int32, (splat_rows, lanes), 0
    )

    def add_products(sums, vectors):
        return tuple(total + vectors[i] * vectors[j] for total, (i, j) in zip(sums, pairs))

    zeros = tuple(jnp.zeros((8, lanes), jnp.float32) for _ in pairs)

    def gram_of(sums, phase):
        for n, total in enumerate(sums):
            red[n : n + 1] = jnp.sum(total, axis=0, keepdims=True)
        mine[phase] = lax.dot_general(
            ones,
            red[...],
            (((1,), (1,)), ((), ())),
            precision=lax.Precision.HIGHEST,
            preferred_element_type=jnp.float32,
        )
        for step in range(1, devices):
            pltpu.make_async_remote_copy(
                src_ref=mine.at[phase, pl.ds(0, 1)],
                dst_ref=slots.at[phase, pl.ds(me, 1)],
                send_sem=gram_send.at[phase],
                recv_sem=gram_recv.at[phase],
                device_id=peer(step),
                device_id_type=MESH,
            ).start()
        slots[phase, pl.ds(me, 1)] = mine[phase, 0:1]
        every = pltpu.make_async_remote_copy(
            src_ref=slots.at[phase, pl.ds(0, devices - 1)],
            dst_ref=slots.at[phase, pl.ds(0, devices - 1)],
            send_sem=gram_send.at[phase],
            recv_sem=gram_recv.at[phase],
            device_id=peer(1),
            device_id_type=MESH,
        )
        every.wait_recv()
        whole = jnp.sum(slots[phase], axis=0, keepdims=True) / total_count
        spread = jnp.where(diagonal, jnp.broadcast_to(whole, diagonal.shape), 0.0)
        splat[...] = jnp.broadcast_to(jnp.sum(spread, axis=1, keepdims=True), spread.shape)
        every.wait_send()
        return {pair: splat[n : n + 1] for n, pair in enumerate(pairs)}

    def factorise(gram):
        left = dict(gram)
        low, inv = {}, {}
        for j in range(count):
            root = jnp.sqrt(left[j, j])
            scale = 1.0 / root
            low[j, j], inv[j, j] = root, scale
            for i in range(j + 1, count):
                low[i, j] = left[i, j] * scale
            for i in range(j + 1, count):
                for k in range(j + 1, i + 1):
                    left[i, k] = left[i, k] - low[i, j] * low[k, j]
        for i in range(count):
            for j in range(i):
                total = low[i, j] * inv[j, j]
                for k in range(j + 1, i):
                    total = total + low[i, k] * inv[k, j]
                inv[i, j] = -(total * inv[i, i])
        for pair, n in place.items():
            lower_inv[n : n + 1] = inv[pair]
        return low

    def combine(vectors):
        results = []
        for i in range(count):
            total = lower_inv[place[i, 0] : place[i, 0] + 1] * vectors[0]
            for j in range(1, i + 1):
                total = total + lower_inv[place[i, j] : place[i, j] + 1] * vectors[j]
            results.append(total)
        return results

    def basis_at(spot, half):
        comp, x = spot
        return [field[BASIS + 2 * n + comp, HALO + x, HALVES[half]] for n in range(count)]

    def spots_of(n):
        comp, x = lax.div(n, rows // 2), lax.rem(n, rows // 2)
        return [(comp, 2 * x + k) for k in range(2)]

    def gram_step(n, sums):
        for spot in spots_of(n):
            for half in range(2):
                sums = add_products(sums, basis_at(spot, half))
        return sums

    low_one = factorise(gram_of(lax.fori_loop(0, rows, gram_step, zeros), 0))

    def ortho_step(n, sums):
        for spot in spots_of(n):
            comp, x = spot
            for half in range(2):
                vectors = combine(basis_at(spot, half))
                for k in range(count):
                    out_ref[k, comp, x, HALVES[half]] = vectors[k]
                sums = add_products(sums, vectors)
        return sums

    low_two = factorise(gram_of(lax.fori_loop(0, rows, ortho_step, zeros), 1))

    fac_row = lax.broadcasted_iota(jnp.int32, (count, count), 0)
    fac_col = lax.broadcasted_iota(jnp.int32, (count, count), 1)
    factor = jnp.zeros((count, count), jnp.float32)
    for i in range(count):
        for j in range(i, count):
            total = low_two[i, i] * low_one[j, i]
            for k in range(i + 1, j + 1):
                total = total + low_two[k, i] * low_one[j, k]
            factor = jnp.where((fac_row == i) & (fac_col == j), total[:, :count], factor)
    factor_ref[...] = factor

    for way in range(2):

        @pl.when(row_ways[way][0])
        def _():
            for part in range(2):
                row_copy(way, part).wait_send()

        @pl.when(side_ways[way][0])
        def _():
            side_copy(way).wait_send()

    for way, side in corners:

        @pl.when(corner_goes(way, side))
        def _():
            corner_copy(way, side).wait_send()


def finish(inverse_ref, basis_ref, factor_in, out_ref, factor_ref):
    count, _, depth, rows, _ = out_ref.shape
    levels = basis_ref.shape[2] // rows
    comp, low = pl.program_id(0), pl.program_id(1) * depth
    factor_ref[...] = factor_in[...]

    def one_level(n):
        spot_row = lax.div(low + n, 2) + 8 * lax.rem(low + n, 2)
        for half in range(rows // 8):
            part = slice(8 * half, 8 * half + 8)
            vectors = [
                basis_ref[n_basis, comp, pl.ds(8 * levels * half + spot_row, 8, stride=levels)]
                for n_basis in range(count)
            ]
            spot = 0
            for i in range(count):
                total = inverse_ref[spot : spot + 1] * vectors[0]
                for j in range(1, i + 1):
                    total = total + inverse_ref[spot + j : spot + j + 1] * vectors[j]
                out_ref[i, 0, n, part] = total
                spot += i + 1

    def some_levels(n, carry):
        for k in range(2):
            one_level(2 * n + k)
        return carry

    lax.fori_loop(0, depth // 2, some_levels, 0)


def on_device(gx_count, gy_count, start_vector, viscosity, friction, shifts):
    levels, rows, lanes = viscosity.shape
    count = shifts.shape[0] + 1
    wide = rows + 2 * HALO
    tiles = (count * (count + 1) // 2 + 7) // 8
    f32 = jnp.float32
    dma = pltpu.SemaphoreType.DMA
    vmem = pl.BlockSpec(memory_space=pltpu.VMEM)
    hbm = pl.BlockSpec(memory_space=pltpu.HBM)
    devices = gx_count * gy_count
    split = (levels // 2, 2, rows, lanes)
    operands = [
        pltpu.with_memory_space_constraint(x, pltpu.HBM)
        for x in (
            start_vector.reshape((2,) + split),
            viscosity.reshape(split),
            friction.reshape(split),
            shifts,
        )
    ]
    ortho_one, factor, inverse = pl.pallas_call(
        functools.partial(kernel, gx_count, gy_count),
        out_shape=(
            jax.ShapeDtypeStruct((count, 2, rows, levels, lanes), f32),
            jax.ShapeDtypeStruct((count, count), f32),
            jax.ShapeDtypeStruct((8 * tiles, lanes), f32),
        ),
        in_specs=[hbm] * 4,
        out_specs=(vmem, vmem, vmem),
        scratch_shapes=[
            pltpu.VMEM((4, 2, levels // 2, rows, lanes), f32),
            pltpu.SMEM(shifts.shape, f32),
            pltpu.VMEM((BASIS + 2 * count, wide, levels, lanes), f32),
            pltpu.VMEM((7, wide, levels, lanes), f32),
            pltpu.VMEM((4, CHUNK, levels, lanes), f32),
            pltpu.VMEM((2, 4, levels, lanes), f32),
            pltpu.VMEM((2, 2, 4, 8, lanes), f32),
            pltpu.VMEM((2, 4, levels, lanes), f32),
            pltpu.VMEM((2, 2, 4, 8, lanes), f32),
            pltpu.VMEM((2, CHUNK, levels, lanes), f32),
            pltpu.VMEM((2, CHUNK, levels, lanes), f32),
            pltpu.VMEM((2, 2, 2, CHUNK + 2, levels, lanes), f32),
            pltpu.VMEM((2, CHUNK + 2, levels, lanes), f32),
            pltpu.VMEM((7, 2, CHUNK, levels, lanes), f32),
            pltpu.VMEM((lanes, lanes), f32),
            pltpu.VMEM((2, 8, lanes), f32),
            pltpu.VMEM((2, devices, lanes), f32),
            pltpu.VMEM((8 * tiles, lanes), f32),
            dma((9,)),
            dma((2, 2)),
            dma((2, 2)),
            dma((2,)),
            dma((2,)),
            dma((2, 2)),
            dma((2, 2)),
            dma((2,)),
            dma((2,)),
        ],
        compiler_params=pltpu.CompilerParams(
            collective_id=0, has_side_effects=True, vmem_limit_bytes=40 * 2**20
        ),
    )(*operands)
    depth = 8
    block = pl.BlockSpec((count, 1, depth, rows, lanes), lambda c, z: (0, c, z, 0, 0))
    return tuple(
        pl.pallas_call(
            finish,
            grid=(2, levels // depth),
            out_shape=(
                jax.ShapeDtypeStruct((count,) + start_vector.shape, f32),
                jax.ShapeDtypeStruct(factor.shape, f32),
            ),
            in_specs=[vmem, vmem, vmem],
            compiler_params=pltpu.CompilerParams(vmem_limit_bytes=12 * 2**20),
            out_specs=(block, pl.BlockSpec(factor.shape, lambda c, z: (0, 0))),
        )(inverse, ortho_one.reshape(count, 2, rows * levels, lanes), factor)
    )


def solution(mesh):
    return jax.shard_map(
        functools.partial(on_device, mesh.shape["gx"], mesh.shape["gy"]),
        mesh=mesh,
        in_specs=(P(None, None, "gx", "gy"), P(None, "gx", "gy"), P(None, "gx", "gy"), P()),
        out_specs=(P(None, None, None, "gx", "gy"), P()),
        check_vma=False,
    )
```

```python
import functools

import jax
import jax.numpy as jnp
from jax import lax
from jax.experimental import pallas as pl
from jax.experimental.pallas import tpu as pltpu
from jax.sharding import PartitionSpec as P

MESH = pl.DeviceIdType.MESH
HALO = 8
GROUP = 2 * HALO
ETA, FRIC, BASIS = 0, 1, 2
CHUNK = 4
NEAR = 4
HALVES = (slice(0, 8), slice(8, 16))


def kernel(
    gx_count,
    gy_count,
    start_hbm,
    eta_hbm,
    fric_hbm,
    shift_hbm,
    out_ref,
    factor_ref,
    lower_inv,
    loaded,
    shift_ref,
    field,
    coef,
    own,
    side_own,
    corner_own,
    beside,
    corner,
    mixed,
    sync,
    pack,
    pack_eta,
    pack_coef,
    red,
    mine,
    slots,
    splat,
    load_sem,
    row_send,
    row_recv,
    side_send,
    side_recv,
    corner_send,
    corner_recv,
    gram_send,
    gram_recv,
):
    f32 = jnp.float32
    powers = shift_hbm.shape[0]
    count = powers + 1
    levels, rows, lanes = field.shape[2], field.shape[1] - 2 * HALO, field.shape[3]
    wide = rows + 2 * HALO
    places = wide // CHUNK
    me_x, me_y = lax.axis_index("gx"), lax.axis_index("gy")
    total_count = 2.0 * levels * rows * lanes * gx_count * gy_count
    devices = gx_count * gy_count
    me = me_x * gy_count + me_y

    def peer(step):
        other = lax.rem(me + step, devices)
        return (lax.div(other, gy_count), lax.rem(other, gy_count))

    loads = [
        pltpu.make_async_copy(src, dst, load_sem.at[n])
        for n, (src, dst) in enumerate(
            (
                (shift_hbm, shift_ref),
                *((eta_hbm.at[:, h], loaded.at[ETA, h]) for h in range(2)),
                *((fric_hbm.at[:, h], loaded.at[FRIC, h]) for h in range(2)),
                *(
                    (start_hbm.at[c, :, h], loaded.at[BASIS + c, h])
                    for c in range(2)
                    for h in range(2)
                ),
            )
        )
    ]
    for load in loads:
        load.start()
    barrier = pltpu.get_barrier_semaphore()
    for step in range(1, devices):
        pl.semaphore_signal(barrier, inc=1, device_id=peer(step), device_id_type=MESH)
    for load in loads:
        load.wait()

    lane = lax.broadcasted_iota(jnp.int32, (8, lanes), 1)
    level = lax.broadcasted_iota(jnp.int32, (8, lanes), 0)
    first, last = level == 0, level == 7
    in_group = lane % GROUP
    place_of = lane // GROUP

    flat = loaded.reshape(4, 2, 8 * rows, lanes)
    for x in range(rows):
        for n in range(4):
            for h in range(2):
                field[n, HALO + x, HALVES[h]] = flat[n, h, pl.ds(x, 8, stride=rows)]

    def turn(value, shift):
        return pltpu.roll(value, shift % lanes, 1)

    def gather(n, spots, tile):
        for half in range(2):
            tiles = tile[half]
            for g, x in spots:
                turned = turn(field[n, x, HALVES[half]], GROUP * g + HALO)
                tiles = jnp.where(place_of == g, turned, tiles)
            yield tiles

    empty = [jnp.zeros((8, lanes), f32)] * 2
    inner_places = range(HALO // CHUNK, (HALO + rows) // CHUNK)
    outer_places = [g for g in range(places) if g not in inner_places]
    folded = {}
    for n in range(4):
        for s in range(CHUNK):
            spots = [(g, CHUNK * g + s) for g in inner_places]
            for half, tile in enumerate(gather(n, spots, empty)):
                own[n, s, HALVES[half]] = tile
        for way in range(2):
            first_row = (rows, HALO)[way]
            spots = [
                (2 * s + k, first_row + CHUNK * k + s) for s in range(CHUNK) for k in range(2)
            ]
            for half, tile in enumerate(gather(n, spots, empty)):
                folded[way, n, half] = tile

    upper_lanes = in_group >= HALO
    inner_lanes = (place_of >= inner_places[0]) & (place_of <= inner_places[-1])
    for n in range(4):
        for half in HALVES:
            two = [
                jnp.where(inner_lanes, own[n, 2 * k, half], turn(own[n, 2 * k + 1, half], lanes // 2))
                for k in range(2)
            ]
            side_own[0, n, half] = jnp.where(upper_lanes, turn(two[1], HALO), two[0])
            side_own[1, n, half] = jnp.where(upper_lanes, two[0], turn(two[1], -HALO))
        for way in range(2):
            one, other = folded[way, n, 0], folded[way, n, 1]
            corner_own[0, way, n] = jnp.where(upper_lanes, turn(other, HALO), one)
            corner_own[1, way, n] = jnp.where(upper_lanes, one, turn(other, -HALO))

    pl.semaphore_wait(barrier, devices - 1)

    up_ok, down_ok = me_x > 0, me_x < gx_count - 1
    left_ok, right_ok = me_y > 0, me_y < gy_count - 1
    row_ways = (
        (down_ok, jnp.minimum(me_x + 1, gx_count - 1), (rows + NEAR, rows), (NEAR, 0)),
        (
            up_ok,
            jnp.maximum(me_x - 1, 0),
            (HALO, HALO + NEAR),
            (HALO + rows, HALO + rows + NEAR),
        ),
    )
    side_ways = (
        (right_ok, jnp.minimum(me_y + 1, gy_count - 1)),
        (left_ok, jnp.maximum(me_y - 1, 0)),
    )

    def row_copy(way, part):
        _, other, src, dst = row_ways[way]
        return pltpu.make_async_remote_copy(
            src_ref=field.at[pl.ds(0, 4), pl.ds(src[part], NEAR)],
            dst_ref=field.at[pl.ds(0, 4), pl.ds(dst[part], NEAR)],
            send_sem=row_send.at[way, part],
            recv_sem=row_recv.at[way, part],
            device_id=(other, me_y),
            device_id_type=MESH,
        )

    def corner_copy(way, side):
        return pltpu.make_async_remote_copy(
            src_ref=corner_own.at[side, way],
            dst_ref=corner.at[side, way],
            send_sem=corner_send.at[side, way],
            recv_sem=corner_recv.at[side, way],
            device_id=(row_ways[way][1], side_ways[side][1]),
            device_id_type=MESH,
        )

    def corner_goes(way, side):
        return row_ways[way][0] & side_ways[side][0]

    corners = [(way, side) for way in range(2) for side in range(2)]

    def side_copy(way):
        return pltpu.make_async_remote_copy(
            src_ref=side_own.at[way],
            dst_ref=beside.at[way],
            send_sem=side_send.at[way],
            recv_sem=side_recv.at[way],
            device_id=(me_x, side_ways[way][1]),
            device_id_type=MESH,
        )

    for part in range(2):
        for way in range(2):

            @pl.when(row_ways[way][0])
            def _():
                row_copy(way, part).start()

    for way in range(2):

        @pl.when(side_ways[way][0])
        def _():
            side_copy(way).start()

    for way, side in corners:

        @pl.when(corner_goes(way, side))
        def _():
            corner_copy(way, side).start()

    def blank(ref, shape):
        ref[ETA] = jnp.zeros(shape, f32)
        ref[FRIC] = jnp.ones(shape, f32)
        for comp in range(2):
            ref[BASIS + comp] = jnp.zeros(shape, f32)

    for way in range(2):

        @pl.when(jnp.logical_not(row_ways[1 - way][0]))
        def _():
            blank(
                field.at[pl.ds(0, 4), pl.ds(min(row_ways[way][3]), HALO)], (HALO, levels, lanes)
            )

        @pl.when(jnp.logical_not(side_ways[1 - way][0]))
        def _():
            blank(beside.at[way], (levels, lanes))

    for way, side in corners:

        @pl.when(jnp.logical_not(corner_goes(1 - way, 1 - side)))
        def _():
            blank(corner.at[side, way], (8, lanes))

    def smooth_levels(even, odd):
        pair = even + odd
        lower = even + jnp.where(first, 0.0, pltpu.roll(odd, 1, 0))
        upper = jnp.where(last, odd, pltpu.roll(lower, 7, 0))
        return pair + lower, pair + upper

    def pairs_of(values):
        return [[a[h] + b[h] for h in range(2)] for a, b in zip(values, values[1:])]

    def coefficients(etas, frics, gates):
        sums = pairs_of(etas)
        results = []
        for r in range(len(frics)):
            smooth = smooth_levels(*[sums[r][h] + sums[r + 1][h] for h in range(2)])
            parts = []
            for h in range(2):
                here, value = etas[r + 1][h], smooth[h]
                around = (value + value) + (turn(value, 1) + turn(value, -1))
                diagonal = frics[r][h] + 6.0 * here + 0.125 * around
                g = (0.125 * gates[r]) / diagonal
                a = here * g
                parts.append(
                    (1.0 + 16.0 * a, a + a, g + g, turn(a, 1), turn(g, 1), turn(a, -1), turn(g, -1))
                )
            results.append(parts)
        return results

    def stream(newton, value, eta, coefs, low, high, store, lag=2):
        def load(r):
            e = eta(r)
            values = [value(c, r) for c in range(2)]
            return values, [[e[h] * v[h] for h in range(2)] for v in values]

        def add(one, two):
            return [[[one[k][c][h] + two[k][c][h] for h in range(2)] for c in range(2)] for k in range(2)]

        def finish_row(r, parts):
            for c in range(2):
                store(c, r, [centre - (up + down) for centre, up, down in parts[c]])

        here = load(low)
        pair = add(load(low - 1), here)
        pending = []
        for r in range(low, high):
            after = load(r + 1)
            next_pair = add(here, after)
            crossed = []
            for c in range(2):
                slope = [next_pair[0][c][h] - pair[0][c][h] for h in range(2)]
                crossed.append([d + d for d in slope])
            parts = []
            for c in range(2):
                plain, weighted = [
                    smooth_levels(*[pair[k][c][h] + next_pair[k][c][h] for h in range(2)])
                    for k in range(2)
                ]
                out = []
                for h in range(2):
                    centre_c, a_mid, g_mid, a_up, g_up, a_down, g_down = coefs(r, h)
                    p, q, cross = plain[h], weighted[h], crossed[1 - c][h]
                    ups = a_up * (p - cross) + g_up * q
                    downs = a_down * (p + cross) + g_down * q
                    up, down = turn(ups, -1), turn(downs, 1)
                    centre = (centre_c - newton) * here[0][c][h] - (a_mid * p + g_mid * q)
                    out.append((centre, up, down))
                parts.append(out)
            pending.append((r, parts))
            if len(pending) > lag:
                finish_row(*pending.pop(0))
            here, pair = after, next_pair
        for r, parts in pending:
            finish_row(r, parts)

    def row_of(ref, n, x):
        return [ref[n, x, half] for half in HALVES]

    def row_coefficients(start, size):
        etas = [row_of(field, ETA, start - 1 + r) for r in range(size + 2)]
        frics = [row_of(field, FRIC, start + r) for r in range(size)]
        gates = []
        for r in range(size):
            x = start + r
            inside = ((x >= HALO) | up_ok) & ((x < rows + HALO) | down_ok)
            gates.append(jnp.where(inside, 1.0, 0.0))
        for r, parts in enumerate(coefficients(etas, frics, gates)):
            for h in range(2):
                for n in range(7):
                    coef[n, start + r, HALVES[h]] = parts[h][n]

    def merged(c, r, h, value):
        turned = turn(mixed[c, r % CHUNK, HALVES[h]], -(GROUP * (r // CHUNK) + HALO))
        return jnp.where(edge, turned, value)

    def main_rows(power, low, high, merging=False):
        before = BASIS + 2 * (power - 1)

        def store(c, r, out):
            for h in range(2):
                result = out[h]
                if merging and HALO <= r < HALO + rows:
                    result = merged(c, r, h, result)
                field[before + 2 + c, r, HALVES[h]] = result

        stream(
            shift_ref[power - 1],
            lambda c, r: row_of(field, before + c, r),
            lambda r: row_of(field, ETA, r),
            lambda r, h: [coef[n, r, HALVES[h]] for n in range(7)],
            low,
            high,
            store,
        )

    def merge(power, low, high):
        for c in range(2):
            for r in range(low, high):
                for h in range(2):
                    spot = BASIS + 2 * power + c
                    field[spot, r, HALVES[h]] = merged(c, r, h, field[spot, r, HALVES[h]])

    row_coefficients(HALO + 1, rows - 2)

    half_way = powers // 2
    edge = (lane < HALO // 2) | (lane >= lanes - HALO // 2)
    for power in range(1, half_way + 1):
        main_rows(power, HALO + power, HALO + rows - power)

    for part in range(2):
        for way in range(2):

            @pl.when(row_ways[1 - way][0])
            def _():
                row_copy(way, part).wait_recv()

        top = (NEAR, 0)[part]
        bottom = rows + 2 * HALO - NEAR - top
        row_coefficients(top + 1, NEAR)
        row_coefficients(bottom - 1, NEAR)
        for power in range(1, half_way + 1):
            main_rows(power, top + power, top + power + NEAR)
            main_rows(power, bottom - power, bottom - power + NEAR)

    for way in range(2):

        @pl.when(side_ways[1 - way][0])
        def _():
            side_copy(way).wait_recv()

    for way, side in corners:

        @pl.when(corner_goes(1 - way, 1 - side))
        def _():
            corner_copy(way, side).wait_recv()

    row_inside = ((place_of >= HALO // CHUNK) | up_ok) & (
        (place_of < (HALO + rows) // CHUNK) | down_ok
    )
    side_inside = (row_inside & ((in_group >= HALO) | left_ok), row_inside & ((in_group < HALO) | right_ok))
    own_part = (in_group >= HALO, in_group < HALO)

    def wrapped(values):
        return (
            [[turn(v, GROUP) for v in values[-1]]]
            + values
            + [[turn(v, -GROUP) for v in values[0]]]
        )

    own_rows = [
        [
            list(
                gather(
                    n, [(g, CHUNK * g + s) for g in outer_places], [own[n, s, half] for half in HALVES]
                )
            )
            for s in range(CHUNK)
        ]
        for n in range(4)
    ]

    def beside_rows(side, n, s, h):
        back = HALO if side else -HALO
        value = turn(beside[side, n, HALVES[h]], (s % 2) * (lanes // 2) + (s // 2) * back)
        for way in range(2):
            place = (0, places - HALO // CHUNK)[way]
            turned = turn(corner[side, way, n], GROUP * (place - 2 * s) + h * back)
            here = (place_of >= place) & (place_of < place + HALO // CHUNK)
            value = jnp.where(here, turned, value)
        return value

    for side in range(2):
        fields = [
            [
                [
                    jnp.where(
                        own_part[side], own_rows[n][s][h], beside_rows(side, n, s, h)
                    )
                    for h in range(2)
                ]
                for s in range(CHUNK)
            ]
            for n in range(4)
        ]
        etas = wrapped(fields[ETA])
        gate = jnp.where(side_inside[side], 1.0, 0.0)
        for r, parts in enumerate(coefficients(etas, fields[FRIC], [gate] * CHUNK)):
            for h in range(2):
                for n in range(7):
                    pack_coef[n, side, r, HALVES[h]] = parts[h][n]
        for r in range(CHUNK + 2):
            for h in range(2):
                pack_eta[side, r, HALVES[h]] = etas[r][h]
        for c in range(2):
            for r, value in enumerate(wrapped(fields[BASIS + c])):
                for h in range(2):
                    pack[0, side, c, r, HALVES[h]] = value[h]

    near = (in_group >= HALO + half_way, in_group < HALO - half_way)

    def pack_power(power):
        now, later = (power - 1) % 2, power % 2
        results = {}
        for side in range(2):

            def store(c, r, out):
                for h in range(2):
                    result = out[h]
                    results[side, c, r, h] = result
                    if side == 1:
                        mixed[c, r - 1, HALVES[h]] = jnp.where(
                            own_part[0], results[0, c, r, h], result
                        )
                    if power == half_way:
                        result = jnp.where(near[side], sync[c, r - 1, HALVES[h]], result)
                    pack[later, side, c, r, HALVES[h]] = result
                    if r == CHUNK:
                        pack[later, side, c, 0, HALVES[h]] = turn(result, GROUP)
                    if r == 1:
                        pack[later, side, c, CHUNK + 1, HALVES[h]] = turn(result, -GROUP)

            stream(
                shift_ref[power - 1],
                lambda c, r: [pack[now, side, c, r, half] for half in HALVES],
                lambda r: [pack_eta[side, r, half] for half in HALVES],
                lambda r, h: [pack_coef[n, side, r - 1, HALVES[h]] for n in range(7)],
                1,
                CHUNK + 1,
                store,
            )

    def make_sync():
        for c in range(2):
            for s in range(CHUNK):
                for half in HALVES:
                    tile = jnp.zeros((8, lanes), f32)
                    for g in range(half_way // CHUNK, (wide - half_way) // CHUNK):
                        turned = turn(
                            field[BASIS + 2 * half_way + c, CHUNK * g + s, half], GROUP * g + HALO
                        )
                        tile = jnp.where(place_of == g, turned, tile)
                    sync[c, s, half] = tile

    for power in range(1, half_way):
        pack_power(power)
        if power == half_way - 1:
            make_sync()
        merge(power, HALO, HALO + rows)
    pack_power(half_way)
    merge(half_way, half_way, wide - half_way)
    for power in range(half_way + 1, powers + 1):
        pack_power(power)
        main_rows(power, power, wide - power, True)

    pairs = [(i, j) for i in range(count) for j in range(i + 1)]
    place = {pair: n for n, pair in enumerate(pairs)}
    padded = red.shape[0]
    red[...] = jnp.zeros((padded, lanes), jnp.float32)
    ones = jnp.ones((8, lanes), jnp.float32)
    splat_rows = splat.shape[0]
    diagonal = lax.broadcasted_iota(jnp.int32, (splat_rows, lanes), 1) == lax.broadcasted_iota(
        jnp.int32, (splat_rows, lanes), 0
    )

    def add_products(sums, vectors):
        return tuple(total + vectors[i] * vectors[j] for total, (i, j) in zip(sums, pairs))

    zeros = tuple(jnp.zeros((8, lanes), jnp.float32) for _ in pairs)

    def gram_of(sums, phase):
        for n, total in enumerate(sums):
            red[n : n + 1] = jnp.sum(total, axis=0, keepdims=True)
        mine[phase] = lax.dot_general(
            ones,
            red[...],
            (((1,), (1,)), ((), ())),
            precision=lax.Precision.HIGHEST,
            preferred_element_type=jnp.float32,
        )
        for step in range(1, devices):
            pltpu.make_async_remote_copy(
                src_ref=mine.at[phase, pl.ds(0, 1)],
                dst_ref=slots.at[phase, pl.ds(me, 1)],
                send_sem=gram_send.at[phase],
                recv_sem=gram_recv.at[phase],
                device_id=peer(step),
                device_id_type=MESH,
            ).start()
        slots[phase, pl.ds(me, 1)] = mine[phase, 0:1]
        every = pltpu.make_async_remote_copy(
            src_ref=slots.at[phase, pl.ds(0, devices - 1)],
            dst_ref=slots.at[phase, pl.ds(0, devices - 1)],
            send_sem=gram_send.at[phase],
            recv_sem=gram_recv.at[phase],
            device_id=peer(1),
            device_id_type=MESH,
        )
        every.wait_recv()
        whole = jnp.sum(slots[phase], axis=0, keepdims=True) / total_count
        spread = jnp.where(diagonal, jnp.broadcast_to(whole, diagonal.shape), 0.0)
        splat[...] = jnp.broadcast_to(jnp.sum(spread, axis=1, keepdims=True), spread.shape)
        every.wait_send()
        return {pair: splat[n : n + 1] for n, pair in enumerate(pairs)}

    def factorise(gram):
        left = dict(gram)
        low, inv = {}, {}
        for j in range(count):
            root = jnp.sqrt(left[j, j])
            scale = 1.0 / root
            low[j, j], inv[j, j] = root, scale
            for i in range(j + 1, count):
                low[i, j] = left[i, j] * scale
            for i in range(j + 1, count):
                for k in range(j + 1, i + 1):
                    left[i, k] = left[i, k] - low[i, j] * low[k, j]
        for i in range(count):
            for j in range(i):
                total = low[i, j] * inv[j, j]
                for k in range(j + 1, i):
                    total = total + low[i, k] * inv[k, j]
                inv[i, j] = -(total * inv[i, i])
        for pair, n in place.items():
            lower_inv[n : n + 1] = inv[pair]
        return low

    def combine(vectors):
        results = []
        for i in range(count):
            total = lower_inv[place[i, 0] : place[i, 0] + 1] * vectors[0]
            for j in range(1, i + 1):
                total = total + lower_inv[place[i, j] : place[i, j] + 1] * vectors[j]
            results.append(total)
        return results

    def basis_at(spot, half):
        comp, x = spot
        return [field[BASIS + 2 * n + comp, HALO + x, HALVES[half]] for n in range(count)]

    def spots_of(n):
        comp, x = lax.div(n, rows // 4), lax.rem(n, rows // 4)
        return [(comp, 4 * x + k) for k in range(4)]

    def gram_step(n, sums):
        for spot in spots_of(n):
            for half in range(2):
                sums = add_products(sums, basis_at(spot, half))
        return sums

    low_one = factorise(gram_of(lax.fori_loop(0, rows // 2, gram_step, zeros), 0))

    def ortho_step(n, sums):
        for spot in spots_of(n):
            comp, x = spot
            for half in range(2):
                vectors = combine(basis_at(spot, half))
                for k in range(count):
                    out_ref[k, comp, x, HALVES[half]] = vectors[k]
                sums = add_products(sums, vectors)
        return sums

    low_two = factorise(gram_of(lax.fori_loop(0, rows // 2, ortho_step, zeros), 1))

    fac_row = lax.broadcasted_iota(jnp.int32, (count, count), 0)
    fac_col = lax.broadcasted_iota(jnp.int32, (count, count), 1)
    factor = jnp.zeros((count, count), jnp.float32)
    for i in range(count):
        for j in range(i, count):
            total = low_two[i, i] * low_one[j, i]
            for k in range(i + 1, j + 1):
                total = total + low_two[k, i] * low_one[j, k]
            factor = jnp.where((fac_row == i) & (fac_col == j), total[:, :count], factor)
    factor_ref[...] = factor

    for way in range(2):

        @pl.when(row_ways[way][0])
        def _():
            for part in range(2):
                row_copy(way, part).wait_send()

        @pl.when(side_ways[way][0])
        def _():
            side_copy(way).wait_send()

    for way, side in corners:

        @pl.when(corner_goes(way, side))
        def _():
            corner_copy(way, side).wait_send()


def finish(inverse_ref, basis_ref, factor_in, out_ref, factor_ref):
    count, _, depth, rows, _ = out_ref.shape
    levels = basis_ref.shape[2] // rows
    comp, low = pl.program_id(0), pl.program_id(1) * depth
    factor_ref[...] = factor_in[...]

    def one_level(n):
        spot_row = lax.div(low + n, 2) + 8 * lax.rem(low + n, 2)
        for half in range(rows // 8):
            part = slice(8 * half, 8 * half + 8)
            vectors = [
                basis_ref[n_basis, comp, pl.ds(8 * levels * half + spot_row, 8, stride=levels)]
                for n_basis in range(count)
            ]
            spot = 0
            for i in range(count):
                total = inverse_ref[spot : spot + 1] * vectors[0]
                for j in range(1, i + 1):
                    total = total + inverse_ref[spot + j : spot + j + 1] * vectors[j]
                out_ref[i, 0, n, part] = total
                spot += i + 1

    def some_levels(n, carry):
        for k in range(4):
            one_level(4 * n + k)
        return carry

    lax.fori_loop(0, depth // 4, some_levels, 0)


def on_device(gx_count, gy_count, start_vector, viscosity, friction, shifts):
    levels, rows, lanes = viscosity.shape
    count = shifts.shape[0] + 1
    wide = rows + 2 * HALO
    tiles = (count * (count + 1) // 2 + 7) // 8
    f32 = jnp.float32
    dma = pltpu.SemaphoreType.DMA
    vmem = pl.BlockSpec(memory_space=pltpu.VMEM)
    hbm = pl.BlockSpec(memory_space=pltpu.HBM)
    devices = gx_count * gy_count
    split = (levels // 2, 2, rows, lanes)
    operands = [
        pltpu.with_memory_space_constraint(x, pltpu.HBM)
        for x in (
            start_vector.reshape((2,) + split),
            viscosity.reshape(split),
            friction.reshape(split),
            shifts,
        )
    ]
    ortho_one, factor, inverse = pl.pallas_call(
        functools.partial(kernel, gx_count, gy_count),
        out_shape=(
            jax.ShapeDtypeStruct((count, 2, rows, levels, lanes), f32),
            jax.ShapeDtypeStruct((count, count), f32),
            jax.ShapeDtypeStruct((8 * tiles, lanes), f32),
        ),
        in_specs=[hbm] * 4,
        out_specs=(vmem, vmem, vmem),
        scratch_shapes=[
            pltpu.VMEM((4, 2, levels // 2, rows, lanes), f32),
            pltpu.SMEM(shifts.shape, f32),
            pltpu.VMEM((BASIS + 2 * count, wide, levels, lanes), f32),
            pltpu.VMEM((7, wide, levels, lanes), f32),
            pltpu.VMEM((4, CHUNK, levels, lanes), f32),
            pltpu.VMEM((2, 4, levels, lanes), f32),
            pltpu.VMEM((2, 2, 4, 8, lanes), f32),
            pltpu.VMEM((2, 4, levels, lanes), f32),
            pltpu.VMEM((2, 2, 4, 8, lanes), f32),
            pltpu.VMEM((2, CHUNK, levels, lanes), f32),
            pltpu.VMEM((2, CHUNK, levels, lanes), f32),
            pltpu.VMEM((2, 2, 2, CHUNK + 2, levels, lanes), f32),
            pltpu.VMEM((2, CHUNK + 2, levels, lanes), f32),
            pltpu.VMEM((7, 2, CHUNK, levels, lanes), f32),
            pltpu.VMEM((lanes, lanes), f32),
            pltpu.VMEM((2, 8, lanes), f32),
            pltpu.VMEM((2, devices, lanes), f32),
            pltpu.VMEM((8 * tiles, lanes), f32),
            dma((9,)),
            dma((2, 2)),
            dma((2, 2)),
            dma((2,)),
            dma((2,)),
            dma((2, 2)),
            dma((2, 2)),
            dma((2,)),
            dma((2,)),
        ],
        compiler_params=pltpu.CompilerParams(
            collective_id=0, has_side_effects=True, vmem_limit_bytes=40 * 2**20
        ),
    )(*operands)
    depth = 8
    block = pl.BlockSpec((count, 1, depth, rows, lanes), lambda c, z: (0, c, z, 0, 0))
    return tuple(
        pl.pallas_call(
            finish,
            grid=(2, levels // depth),
            out_shape=(
                jax.ShapeDtypeStruct((count,) + start_vector.shape, f32),
                jax.ShapeDtypeStruct(factor.shape, f32),
            ),
            in_specs=[vmem, vmem, vmem],
            compiler_params=pltpu.CompilerParams(vmem_limit_bytes=12 * 2**20),
            out_specs=(block, pl.BlockSpec(factor.shape, lambda c, z: (0, 0))),
        )(inverse, ortho_one.reshape(count, 2, rows * levels, lanes), factor)
    )


def solution(mesh):
    return jax.shard_map(
        functools.partial(on_device, mesh.shape["gx"], mesh.shape["gy"]),
        mesh=mesh,
        in_specs=(P(None, None, "gx", "gy"), P(None, "gx", "gy"), P(None, "gx", "gy"), P()),
        out_specs=(P(None, None, None, "gx", "gy"), P()),
        check_vma=False,
    )
```

```python
import functools

import jax
import jax.numpy as jnp
from jax import lax
from jax.experimental import pallas as pl
from jax.experimental.pallas import tpu as pltpu
from jax.sharding import PartitionSpec as P

MESH = pl.DeviceIdType.MESH
HALO = 8
GROUP = 2 * HALO
ETA, FRIC, BASIS = 0, 1, 2
CHUNK = 4
NEAR = 4
HALVES = (slice(0, 8), slice(8, 16))


def kernel(
    gx_count,
    gy_count,
    start_hbm,
    eta_hbm,
    fric_hbm,
    shift_hbm,
    out_ref,
    factor_ref,
    lower_inv,
    loaded,
    shift_ref,
    field,
    coef,
    own,
    side_own,
    corner_own,
    beside,
    corner,
    mixed,
    sync,
    pack,
    pack_eta,
    pack_coef,
    red,
    mine,
    slots,
    splat,
    load_sem,
    row_send,
    row_recv,
    side_send,
    side_recv,
    corner_send,
    corner_recv,
    gram_send,
    gram_recv,
):
    f32 = jnp.float32
    powers = shift_hbm.shape[0]
    count = powers + 1
    levels, rows, lanes = field.shape[2], field.shape[1] - 2 * HALO, field.shape[3]
    wide = rows + 2 * HALO
    places = wide // CHUNK
    me_x, me_y = lax.axis_index("gx"), lax.axis_index("gy")
    total_count = 2.0 * levels * rows * lanes * gx_count * gy_count
    devices = gx_count * gy_count
    me = me_x * gy_count + me_y

    def reach(offset):
        return min(offset[1], gy_count - offset[1]) + min(offset[0], gx_count - offset[0])

    offsets = [(dx, dy) for dx in range(gx_count) for dy in range(gy_count) if dx or dy]
    offsets.sort(key=lambda offset: -reach(offset))

    def peer(offset):
        return (lax.rem(me_x + offset[0], gx_count), lax.rem(me_y + offset[1], gy_count))

    loads = [
        pltpu.make_async_copy(src, dst, load_sem.at[n])
        for n, (src, dst) in enumerate(
            (
                (shift_hbm, shift_ref),
                *((eta_hbm.at[:, h], loaded.at[ETA, h]) for h in range(2)),
                *((fric_hbm.at[:, h], loaded.at[FRIC, h]) for h in range(2)),
                *(
                    (start_hbm.at[c, :, h], loaded.at[BASIS + c, h])
                    for c in range(2)
                    for h in range(2)
                ),
            )
        )
    ]
    for load in loads:
        load.start()
    barrier = pltpu.get_barrier_semaphore()
    for offset in offsets:
        pl.semaphore_signal(barrier, inc=1, device_id=peer(offset), device_id_type=MESH)
    for load in loads:
        load.wait()

    lane = lax.broadcasted_iota(jnp.int32, (8, lanes), 1)
    level = lax.broadcasted_iota(jnp.int32, (8, lanes), 0)
    first, last = level == 0, level == 7
    in_group = lane % GROUP
    place_of = lane // GROUP

    flat = loaded.reshape(4, 2, 8 * rows, lanes)
    for x in range(rows):
        for n in range(4):
            for h in range(2):
                field[n, HALO + x, HALVES[h]] = flat[n, h, pl.ds(x, 8, stride=rows)]

    def turn(value, shift):
        return pltpu.roll(value, shift % lanes, 1)

    def gather(n, spots, tile):
        for half in range(2):
            tiles = tile[half]
            for g, x in spots:
                turned = turn(field[n, x, HALVES[half]], GROUP * g + HALO)
                tiles = jnp.where(place_of == g, turned, tiles)
            yield tiles

    empty = [jnp.zeros((8, lanes), f32)] * 2
    inner_places = range(HALO // CHUNK, (HALO + rows) // CHUNK)
    outer_places = [g for g in range(places) if g not in inner_places]
    folded = {}
    for n in range(4):
        for s in range(CHUNK):
            spots = [(g, CHUNK * g + s) for g in inner_places]
            for half, tile in enumerate(gather(n, spots, empty)):
                own[n, s, HALVES[half]] = tile
        for way in range(2):
            first_row = (rows, HALO)[way]
            spots = [
                (2 * s + k, first_row + CHUNK * k + s) for s in range(CHUNK) for k in range(2)
            ]
            for half, tile in enumerate(gather(n, spots, empty)):
                folded[way, n, half] = tile

    upper_lanes = in_group >= HALO
    inner_lanes = (place_of >= inner_places[0]) & (place_of <= inner_places[-1])
    for n in range(4):
        for half in HALVES:
            two = [
                jnp.where(inner_lanes, own[n, 2 * k, half], turn(own[n, 2 * k + 1, half], lanes // 2))
                for k in range(2)
            ]
            side_own[0, n, half] = jnp.where(upper_lanes, turn(two[1], HALO), two[0])
            side_own[1, n, half] = jnp.where(upper_lanes, two[0], turn(two[1], -HALO))
        for way in range(2):
            one, other = folded[way, n, 0], folded[way, n, 1]
            corner_own[0, way, n] = jnp.where(upper_lanes, turn(other, HALO), one)
            corner_own[1, way, n] = jnp.where(upper_lanes, one, turn(other, -HALO))

    pl.semaphore_wait(barrier, devices - 1)

    up_ok, down_ok = me_x > 0, me_x < gx_count - 1
    left_ok, right_ok = me_y > 0, me_y < gy_count - 1
    row_ways = (
        (down_ok, jnp.minimum(me_x + 1, gx_count - 1), (rows + NEAR, rows), (NEAR, 0)),
        (
            up_ok,
            jnp.maximum(me_x - 1, 0),
            (HALO, HALO + NEAR),
            (HALO + rows, HALO + rows + NEAR),
        ),
    )
    side_ways = (
        (right_ok, jnp.minimum(me_y + 1, gy_count - 1)),
        (left_ok, jnp.maximum(me_y - 1, 0)),
    )

    def row_copy(way, part):
        _, other, src, dst = row_ways[way]
        return pltpu.make_async_remote_copy(
            src_ref=field.at[pl.ds(0, 4), pl.ds(src[part], NEAR)],
            dst_ref=field.at[pl.ds(0, 4), pl.ds(dst[part], NEAR)],
            send_sem=row_send.at[way, part],
            recv_sem=row_recv.at[way, part],
            device_id=(other, me_y),
            device_id_type=MESH,
        )

    def corner_copy(way, side):
        return pltpu.make_async_remote_copy(
            src_ref=corner_own.at[side, way],
            dst_ref=corner.at[side, way],
            send_sem=corner_send.at[side, way],
            recv_sem=corner_recv.at[side, way],
            device_id=(row_ways[way][1], side_ways[side][1]),
            device_id_type=MESH,
        )

    def corner_goes(way, side):
        return row_ways[way][0] & side_ways[side][0]

    corners = [(way, side) for way in range(2) for side in range(2)]

    def side_copy(way):
        return pltpu.make_async_remote_copy(
            src_ref=side_own.at[way],
            dst_ref=beside.at[way],
            send_sem=side_send.at[way],
            recv_sem=side_recv.at[way],
            device_id=(me_x, side_ways[way][1]),
            device_id_type=MESH,
        )

    for part in range(2):
        for way in range(2):

            @pl.when(row_ways[way][0])
            def _():
                row_copy(way, part).start()

    for way in range(2):

        @pl.when(side_ways[way][0])
        def _():
            side_copy(way).start()

    for way, side in corners:

        @pl.when(corner_goes(way, side))
        def _():
            corner_copy(way, side).start()

    def blank(ref, shape):
        ref[ETA] = jnp.zeros(shape, f32)
        ref[FRIC] = jnp.ones(shape, f32)
        for comp in range(2):
            ref[BASIS + comp] = jnp.zeros(shape, f32)

    for way in range(2):

        @pl.when(jnp.logical_not(row_ways[1 - way][0]))
        def _():
            blank(
                field.at[pl.ds(0, 4), pl.ds(min(row_ways[way][3]), HALO)], (HALO, levels, lanes)
            )

        @pl.when(jnp.logical_not(side_ways[1 - way][0]))
        def _():
            blank(beside.at[way], (levels, lanes))

    for way, side in corners:

        @pl.when(jnp.logical_not(corner_goes(1 - way, 1 - side)))
        def _():
            blank(corner.at[side, way], (8, lanes))

    def smooth_levels(even, odd):
        pair = even + odd
        lower = even + jnp.where(first, 0.0, pltpu.roll(odd, 1, 0))
        upper = jnp.where(last, odd, pltpu.roll(lower, 7, 0))
        return pair + lower, pair + upper

    def pairs_of(values):
        return [[a[h] + b[h] for h in range(2)] for a, b in zip(values, values[1:])]

    def coefficients(etas, frics, gates):
        sums = pairs_of(etas)
        results = []
        for r in range(len(frics)):
            smooth = smooth_levels(*[sums[r][h] + sums[r + 1][h] for h in range(2)])
            parts = []
            for h in range(2):
                here, value = etas[r + 1][h], smooth[h]
                around = (value + value) + (turn(value, 1) + turn(value, -1))
                diagonal = frics[r][h] + 6.0 * here + 0.125 * around
                g = (0.125 * gates[r]) / diagonal
                a = here * g
                parts.append(
                    (1.0 + 16.0 * a, a + a, g + g, turn(a, 1), turn(g, 1), turn(a, -1), turn(g, -1))
                )
            results.append(parts)
        return results

    def stream(newton, value, eta, coefs, low, high, store, lag=2):
        def load(r):
            e = eta(r)
            values = [value(c, r) for c in range(2)]
            return values, [[e[h] * v[h] for h in range(2)] for v in values]

        def add(one, two):
            return [[[one[k][c][h] + two[k][c][h] for h in range(2)] for c in range(2)] for k in range(2)]

        def finish_row(r, parts):
            for c in range(2):
                store(c, r, [centre - (up + down) for centre, up, down in parts[c]])

        here = load(low)
        pair = add(load(low - 1), here)
        pending = []
        for r in range(low, high):
            after = load(r + 1)
            next_pair = add(here, after)
            crossed = []
            for c in range(2):
                slope = [next_pair[0][c][h] - pair[0][c][h] for h in range(2)]
                crossed.append([d + d for d in slope])
            parts = []
            for c in range(2):
                plain, weighted = [
                    smooth_levels(*[pair[k][c][h] + next_pair[k][c][h] for h in range(2)])
                    for k in range(2)
                ]
                out = []
                for h in range(2):
                    centre_c, a_mid, g_mid, a_up, g_up, a_down, g_down = coefs(r, h)
                    p, q, cross = plain[h], weighted[h], crossed[1 - c][h]
                    ups = a_up * (p - cross) + g_up * q
                    downs = a_down * (p + cross) + g_down * q
                    up, down = turn(ups, -1), turn(downs, 1)
                    centre = (centre_c - newton) * here[0][c][h] - (a_mid * p + g_mid * q)
                    out.append((centre, up, down))
                parts.append(out)
            pending.append((r, parts))
            if len(pending) > lag:
                finish_row(*pending.pop(0))
            here, pair = after, next_pair
        for r, parts in pending:
            finish_row(r, parts)

    def row_of(ref, n, x):
        return [ref[n, x, half] for half in HALVES]

    def row_coefficients(start, size):
        etas = [row_of(field, ETA, start - 1 + r) for r in range(size + 2)]
        frics = [row_of(field, FRIC, start + r) for r in range(size)]
        gates = []
        for r in range(size):
            x = start + r
            inside = ((x >= HALO) | up_ok) & ((x < rows + HALO) | down_ok)
            gates.append(jnp.where(inside, 1.0, 0.0))
        for r, parts in enumerate(coefficients(etas, frics, gates)):
            for h in range(2):
                for n in range(7):
                    coef[n, start + r, HALVES[h]] = parts[h][n]

    def merged(power, c, r, h, value):
        turned = turn(mixed[power, c, r % CHUNK, HALVES[h]], -(GROUP * (r // CHUNK) + HALO))
        return jnp.where(edge, turned, value)

    def main_rows(power, low, high, merging=False):
        before = BASIS + 2 * (power - 1)

        def store(c, r, out):
            for h in range(2):
                result = out[h]
                if merging and HALO <= r < HALO + rows:
                    result = merged(power, c, r, h, result)
                field[before + 2 + c, r, HALVES[h]] = result

        stream(
            shift_ref[power - 1],
            lambda c, r: row_of(field, before + c, r),
            lambda r: row_of(field, ETA, r),
            lambda r, h: [coef[n, r, HALVES[h]] for n in range(7)],
            low,
            high,
            store,
        )

    def merge(power, low, high):
        for c in range(2):
            for r in range(low, high):
                for h in range(2):
                    spot = BASIS + 2 * power + c
                    field[spot, r, HALVES[h]] = merged(power, c, r, h, field[spot, r, HALVES[h]])

    row_coefficients(HALO + 1, rows - 2)

    half_way = powers // 2
    edge = (lane < HALO // 2) | (lane >= lanes - HALO // 2)
    for power in range(1, half_way + 1):
        main_rows(power, HALO + power, HALO + rows - power)

    for part in range(2):
        for way in range(2):

            @pl.when(row_ways[1 - way][0])
            def _():
                row_copy(way, part).wait_recv()

        if part == 0:
            row_coefficients(NEAR + 1, NEAR)
            row_coefficients(rows + HALO - 1, NEAR)
            for power in range(1, half_way + 1):
                main_rows(power, NEAR + power, NEAR + power + NEAR)
                main_rows(power, rows + HALO - power, rows + HALO - power + NEAR)

    for way in range(2):

        @pl.when(side_ways[1 - way][0])
        def _():
            side_copy(way).wait_recv()

    for way, side in corners:

        @pl.when(corner_goes(1 - way, 1 - side))
        def _():
            corner_copy(way, side).wait_recv()

    far = wide - NEAR
    row_coefficients(1, NEAR)
    row_coefficients(far - 1, NEAR)

    row_inside = ((place_of >= HALO // CHUNK) | up_ok) & (
        (place_of < (HALO + rows) // CHUNK) | down_ok
    )
    side_inside = (row_inside & ((in_group >= HALO) | left_ok), row_inside & ((in_group < HALO) | right_ok))
    own_part = (in_group >= HALO, in_group < HALO)

    def wrapped(values):
        return (
            [[turn(v, GROUP) for v in values[-1]]]
            + values
            + [[turn(v, -GROUP) for v in values[0]]]
        )

    own_rows = [
        [
            list(
                gather(
                    n, [(g, CHUNK * g + s) for g in outer_places], [own[n, s, half] for half in HALVES]
                )
            )
            for s in range(CHUNK)
        ]
        for n in range(4)
    ]

    def beside_rows(side, n, s, h):
        back = HALO if side else -HALO
        value = turn(beside[side, n, HALVES[h]], (s % 2) * (lanes // 2) + (s // 2) * back)
        for way in range(2):
            place = (0, places - HALO // CHUNK)[way]
            turned = turn(corner[side, way, n], GROUP * (place - 2 * s) + h * back)
            here = (place_of >= place) & (place_of < place + HALO // CHUNK)
            value = jnp.where(here, turned, value)
        return value

    for side in range(2):
        fields = [
            [
                [
                    jnp.where(
                        own_part[side], own_rows[n][s][h], beside_rows(side, n, s, h)
                    )
                    for h in range(2)
                ]
                for s in range(CHUNK)
            ]
            for n in range(4)
        ]
        etas = wrapped(fields[ETA])
        gate = jnp.where(side_inside[side], 1.0, 0.0)
        for r, parts in enumerate(coefficients(etas, fields[FRIC], [gate] * CHUNK)):
            for h in range(2):
                for n in range(7):
                    pack_coef[n, side, r, HALVES[h]] = parts[h][n]
        for r in range(CHUNK + 2):
            for h in range(2):
                pack_eta[side, r, HALVES[h]] = etas[r][h]
        for c in range(2):
            for r, value in enumerate(wrapped(fields[BASIS + c])):
                for h in range(2):
                    pack[0, side, c, r, HALVES[h]] = value[h]

    near = (in_group >= HALO + half_way, in_group < HALO - half_way)

    def pack_power(power):
        now, later = (power - 1) % 2, power % 2
        results = {}
        for side in range(2):

            def store(c, r, out):
                for h in range(2):
                    result = out[h]
                    results[side, c, r, h] = result
                    if side == 1:
                        mixed[power, c, r - 1, HALVES[h]] = jnp.where(
                            own_part[0], results[0, c, r, h], result
                        )
                    if power == half_way:
                        result = jnp.where(near[side], sync[c, r - 1, HALVES[h]], result)
                    pack[later, side, c, r, HALVES[h]] = result
                    if r == CHUNK:
                        pack[later, side, c, 0, HALVES[h]] = turn(result, GROUP)
                    if r == 1:
                        pack[later, side, c, CHUNK + 1, HALVES[h]] = turn(result, -GROUP)

            stream(
                shift_ref[power - 1],
                lambda c, r: [pack[now, side, c, r, half] for half in HALVES],
                lambda r: [pack_eta[side, r, half] for half in HALVES],
                lambda r, h: [pack_coef[n, side, r - 1, HALVES[h]] for n in range(7)],
                1,
                CHUNK + 1,
                store,
            )

    def make_sync():
        for c in range(2):
            for s in range(CHUNK):
                for half in HALVES:
                    tile = jnp.zeros((8, lanes), f32)
                    for g in range(half_way // CHUNK, (wide - half_way) // CHUNK):
                        turned = turn(
                            field[BASIS + 2 * half_way + c, CHUNK * g + s, half], GROUP * g + HALO
                        )
                        tile = jnp.where(place_of == g, turned, tile)
                    sync[c, s, half] = tile

    for power in range(1, half_way + 1):
        main_rows(power, power, power + NEAR)
        main_rows(power, far - power, wide - power)
        if power == half_way:
            make_sync()
        pack_power(power)
    merge(half_way, half_way, wide - half_way)
    for power in range(half_way + 1, powers + 1):
        pack_power(power)
        main_rows(power, power, wide - power, True)
        if power - half_way < half_way:
            merge(power - half_way, HALO, HALO + rows)

    pairs = [(i, j) for i in range(count) for j in range(i + 1)]
    place = {pair: n for n, pair in enumerate(pairs)}
    padded = red.shape[0]
    red[...] = jnp.zeros((padded, lanes), jnp.float32)
    ones = jnp.ones((8, lanes), jnp.float32)
    splat_rows = splat.shape[0]
    diagonal = lax.broadcasted_iota(jnp.int32, (splat_rows, lanes), 1) == lax.broadcasted_iota(
        jnp.int32, (splat_rows, lanes), 0
    )

    def add_products(sums, vectors):
        return tuple(total + vectors[i] * vectors[j] for total, (i, j) in zip(sums, pairs))

    zeros = tuple(jnp.zeros((8, lanes), jnp.float32) for _ in pairs)

    def gram_of(sums, phase):
        for n, total in enumerate(sums):
            red[n : n + 1] = jnp.sum(total, axis=0, keepdims=True)
        mine[phase] = lax.dot_general(
            ones,
            red[...],
            (((1,), (1,)), ((), ())),
            precision=lax.Precision.HIGHEST,
            preferred_element_type=jnp.float32,
        )
        for offset in offsets:
            pltpu.make_async_remote_copy(
                src_ref=mine.at[phase, pl.ds(0, 1)],
                dst_ref=slots.at[phase, pl.ds(me, 1)],
                send_sem=gram_send.at[phase],
                recv_sem=gram_recv.at[phase],
                device_id=peer(offset),
                device_id_type=MESH,
            ).start()
        slots[phase, pl.ds(me, 1)] = mine[phase, 0:1]
        every = pltpu.make_async_remote_copy(
            src_ref=slots.at[phase, pl.ds(0, devices - 1)],
            dst_ref=slots.at[phase, pl.ds(0, devices - 1)],
            send_sem=gram_send.at[phase],
            recv_sem=gram_recv.at[phase],
            device_id=peer(offsets[0]),
            device_id_type=MESH,
        )
        every.wait_recv()
        whole = jnp.sum(slots[phase], axis=0, keepdims=True) / total_count
        spread = jnp.where(diagonal, jnp.broadcast_to(whole, diagonal.shape), 0.0)
        splat[...] = jnp.broadcast_to(jnp.sum(spread, axis=1, keepdims=True), spread.shape)
        every.wait_send()
        return {pair: splat[n : n + 1] for n, pair in enumerate(pairs)}

    def factorise(gram):
        left = dict(gram)
        low, inv = {}, {}
        for j in range(count):
            root = jnp.sqrt(left[j, j])
            scale = 1.0 / root
            low[j, j], inv[j, j] = root, scale
            for i in range(j + 1, count):
                low[i, j] = left[i, j] * scale
            for i in range(j + 1, count):
                for k in range(j + 1, i + 1):
                    left[i, k] = left[i, k] - low[i, j] * low[k, j]
        for i in range(count):
            for j in range(i):
                total = low[i, j] * inv[j, j]
                for k in range(j + 1, i):
                    total = total + low[i, k] * inv[k, j]
                inv[i, j] = -(total * inv[i, i])
        for pair, n in place.items():
            lower_inv[n : n + 1] = inv[pair]
        return low

    def combine(vectors):
        results = []
        for i in range(count):
            total = lower_inv[place[i, 0] : place[i, 0] + 1] * vectors[0]
            for j in range(1, i + 1):
                total = total + lower_inv[place[i, j] : place[i, j] + 1] * vectors[j]
            results.append(total)
        return results

    def basis_at(spot, half):
        comp, x = spot
        return [field[BASIS + 2 * n + comp, HALO + x, HALVES[half]] for n in range(count)]

    def spots_of(n):
        comp, x = lax.div(n, rows // 4), lax.rem(n, rows // 4)
        return [(comp, 4 * x + k) for k in range(4)]

    def gram_step(n, sums):
        for spot in spots_of(n):
            for half in range(2):
                sums = add_products(sums, basis_at(spot, half))
        return sums

    low_one = factorise(gram_of(lax.fori_loop(0, rows // 2, gram_step, zeros), 0))

    def ortho_step(n, sums):
        for spot in spots_of(n):
            comp, x = spot
            for half in range(2):
                vectors = combine(basis_at(spot, half))
                for k in range(count):
                    out_ref[k, comp, x, HALVES[half]] = vectors[k]
                sums = add_products(sums, vectors)
        return sums

    low_two = factorise(gram_of(lax.fori_loop(0, rows // 2, ortho_step, zeros), 1))

    fac_row = lax.broadcasted_iota(jnp.int32, (count, count), 0)
    fac_col = lax.broadcasted_iota(jnp.int32, (count, count), 1)
    factor = jnp.zeros((count, count), jnp.float32)
    for i in range(count):
        for j in range(i, count):
            total = low_two[i, i] * low_one[j, i]
            for k in range(i + 1, j + 1):
                total = total + low_two[k, i] * low_one[j, k]
            factor = jnp.where((fac_row == i) & (fac_col == j), total[:, :count], factor)
    factor_ref[...] = factor

    for way in range(2):

        @pl.when(row_ways[way][0])
        def _():
            for part in range(2):
                row_copy(way, part).wait_send()

        @pl.when(side_ways[way][0])
        def _():
            side_copy(way).wait_send()

    for way, side in corners:

        @pl.when(corner_goes(way, side))
        def _():
            corner_copy(way, side).wait_send()


def finish(inverse_ref, basis_ref, factor_in, out_ref, factor_ref):
    count, _, depth, rows, _ = out_ref.shape
    levels = basis_ref.shape[2] // rows
    comp, low = pl.program_id(0), pl.program_id(1) * depth
    factor_ref[...] = factor_in[...]

    def one_level(n):
        spot_row = lax.div(low + n, 2) + 8 * lax.rem(low + n, 2)
        for half in range(rows // 8):
            part = slice(8 * half, 8 * half + 8)
            vectors = [
                basis_ref[n_basis, comp, pl.ds(8 * levels * half + spot_row, 8, stride=levels)]
                for n_basis in range(count)
            ]
            spot = 0
            for i in range(count):
                total = inverse_ref[spot : spot + 1] * vectors[0]
                for j in range(1, i + 1):
                    total = total + inverse_ref[spot + j : spot + j + 1] * vectors[j]
                out_ref[i, 0, n, part] = total
                spot += i + 1

    def some_levels(n, carry):
        for k in range(4):
            one_level(4 * n + k)
        return carry

    lax.fori_loop(0, depth // 4, some_levels, 0)


def on_device(gx_count, gy_count, start_vector, viscosity, friction, shifts):
    levels, rows, lanes = viscosity.shape
    count = shifts.shape[0] + 1
    wide = rows + 2 * HALO
    tiles = (count * (count + 1) // 2 + 7) // 8
    f32 = jnp.float32
    dma = pltpu.SemaphoreType.DMA
    vmem = pl.BlockSpec(memory_space=pltpu.VMEM)
    hbm = pl.BlockSpec(memory_space=pltpu.HBM)
    devices = gx_count * gy_count
    split = (levels // 2, 2, rows, lanes)
    operands = [
        pltpu.with_memory_space_constraint(x, pltpu.HBM)
        for x in (
            start_vector.reshape((2,) + split),
            viscosity.reshape(split),
            friction.reshape(split),
            shifts,
        )
    ]
    ortho_one, factor, inverse = pl.pallas_call(
        functools.partial(kernel, gx_count, gy_count),
        out_shape=(
            jax.ShapeDtypeStruct((count, 2, rows, levels, lanes), f32),
            jax.ShapeDtypeStruct((count, count), f32),
            jax.ShapeDtypeStruct((8 * tiles, lanes), f32),
        ),
        in_specs=[hbm] * 4,
        out_specs=(vmem, vmem, vmem),
        scratch_shapes=[
            pltpu.VMEM((4, 2, levels // 2, rows, lanes), f32),
            pltpu.SMEM(shifts.shape, f32),
            pltpu.VMEM((BASIS + 2 * count, wide, levels, lanes), f32),
            pltpu.VMEM((7, wide, levels, lanes), f32),
            pltpu.VMEM((4, CHUNK, levels, lanes), f32),
            pltpu.VMEM((2, 4, levels, lanes), f32),
            pltpu.VMEM((2, 2, 4, 8, lanes), f32),
            pltpu.VMEM((2, 4, levels, lanes), f32),
            pltpu.VMEM((2, 2, 4, 8, lanes), f32),
            pltpu.VMEM((count, 2, CHUNK, levels, lanes), f32),
            pltpu.VMEM((2, CHUNK, levels, lanes), f32),
            pltpu.VMEM((2, 2, 2, CHUNK + 2, levels, lanes), f32),
            pltpu.VMEM((2, CHUNK + 2, levels, lanes), f32),
            pltpu.VMEM((7, 2, CHUNK, levels, lanes), f32),
            pltpu.VMEM((lanes, lanes), f32),
            pltpu.VMEM((2, 8, lanes), f32),
            pltpu.VMEM((2, devices, lanes), f32),
            pltpu.VMEM((8 * tiles, lanes), f32),
            dma((9,)),
            dma((2, 2)),
            dma((2, 2)),
            dma((2,)),
            dma((2,)),
            dma((2, 2)),
            dma((2, 2)),
            dma((2,)),
            dma((2,)),
        ],
        compiler_params=pltpu.CompilerParams(
            collective_id=0, has_side_effects=True, vmem_limit_bytes=40 * 2**20
        ),
    )(*operands)
    depth = levels
    block = pl.BlockSpec((count, 1, depth, rows, lanes), lambda c, z: (0, c, z, 0, 0))
    return tuple(
        pl.pallas_call(
            finish,
            grid=(2, levels // depth),
            out_shape=(
                jax.ShapeDtypeStruct((count,) + start_vector.shape, f32),
                jax.ShapeDtypeStruct(factor.shape, f32),
            ),
            in_specs=[vmem, vmem, vmem],
            compiler_params=pltpu.CompilerParams(vmem_limit_bytes=12 * 2**20),
            out_specs=(block, pl.BlockSpec(factor.shape, lambda c, z: (0, 0))),
        )(inverse, ortho_one.reshape(count, 2, rows * levels, lanes), factor)
    )


def solution(mesh):
    return jax.shard_map(
        functools.partial(on_device, mesh.shape["gx"], mesh.shape["gy"]),
        mesh=mesh,
        in_specs=(P(None, None, "gx", "gy"), P(None, "gx", "gy"), P(None, "gx", "gy"), P()),
        out_specs=(P(None, None, None, "gx", "gy"), P()),
        check_vma=False,
    )
```
